256 devices in a mesh: layer: 64 (over z, y_lo, x), strip: 4 (over y_hi, core).
Axes of the slice: x: 4, y: 4 (y_hi: 2, y_lo: 2; y = y_hi * 2 + y_lo), z: 8, core: 2. Of those that a mesh axis runs over, the one named last changes fastest.
Arguments:
- probes: float32 [16, 2, 128, 16384], P(None, None, 'layer', 'strip'), may hold values from -6 to 6
- slowness: float32 [128, 16384], P('layer', 'strip'), may hold values from 0.05 to 0.5
- absorbing: int32 [128], P('layer'), may hold values 0 or 1
- partition: int32 [16384], replicated, may hold values from 0 to 16383, each once
Outputs:
- field: float32 [16, 2, 128, 16384], P(None, None, 'layer', 'strip')
- bases: float32 [256, 2, 32, 64], P(('layer', 'strip'))
The draws below stay inside these ranges and needn't reach their ends.
Inputs may be any that keep to these rules, and one draw needn't show every extreme that they name: `partition`: each interface point appears exactly once.
All inputs are finite; a program needn't handle non-finite values. No bound on the sum of `absorbing` on one device may be relied on, other than what follows from the above.
Results may differ from the reference program's by a relative error of at most 0.00013.
Values sent between devices are 32-bit elements; how exact they have to be, the bound alone decides.
A program may use at most 128 MiB of HBM per device.

```python
import math
import jax
import jax.numpy as jnp
from jax import lax

NY = 16384
PROBES = 16
ITERS = 9
BS = 64
NX = 128
NB = 256


def place_ends(result, own_key, smallest, largest):
    spot = [jax.random.randint(jax.random.fold_in(own_key, axis), (), 0, length) for axis, length in enumerate(result.shape)]
    widest = result.shape.index(max(result.shape))
    beside = spot[:widest] + [(spot[widest] + 1) % result.shape[widest]] + spot[widest + 1:]
    return result.at[tuple(spot)].set(smallest).at[tuple(beside)].set(largest)


def levels(rng, extent, cuts, low, high):
    level = 1.0
    for axis_at, shards_of in cuts:
        draws = jax.random.uniform(jax.random.fold_in(jax.random.fold_in(rng, 6), axis_at), (shards_of,), jnp.float32, low / len(cuts), high / len(cuts))
        level = level * jnp.repeat(jnp.exp(draws), extent[axis_at] // shards_of).reshape((-1,) + (1,) * (len(extent) - 1 - axis_at))
    return level


def bell_draw(own_key, dims, width, limit, split=(), kind=jnp.bfloat16):
    drawn = width * jax.random.normal(own_key, dims, jnp.float32)
    if split:
        drawn = drawn * levels(own_key, dims, split, -0.22, 0.18)
    return jnp.clip(drawn, -limit, limit).astype(kind)


def setup_inputs(seed: int = 0) -> dict:
    keys = jax.random.split(jax.random.key(seed), 5)
    probes = bell_draw(keys[0], (PROBES, 2, NX, NY), 1.0, 6.0, ((2, 64), (3, 4)), jnp.float32)
    slowness = jnp.clip(jnp.exp(math.log(0.5) - 2.3025851 * jax.random.uniform(keys[1], (NX, NY), jnp.float32) ** levels(keys[1], (NX, NY), ((0, 64), (1, 4)), -0.2, 0.2)), 0.05, 0.5)
    absorbing = place_ends((jax.random.randint(keys[2], (NX,), 0, 4) < 1).astype(jnp.int32), jax.random.fold_in(keys[2], 1), 0, 1)
    partition = jax.random.permutation(keys[3], NY).astype(jnp.int32)
    return dict(probes=probes, slowness=slowness, absorbing=absorbing, partition=partition)


OMEGA = 0.8
BETA = 0.5
SIGMA = 1.5

def coefficients(slowness, absorbing):
    flags = absorbing.astype(jnp.float32)[:, None]
    dre = 4.0 - slowness
    dim = BETA * slowness + SIGMA * flags
    mag = dre * dre + dim * dim
    return (dre, dim, dre / mag, -dim / mag)

def relax(upad, source, dre, dim, ire, iim):
    nbr = upad[..., :-2, 1:-1] + upad[..., 2:, 1:-1] + upad[..., 1:-1, :-2] + upad[..., 1:-1, 2:]
    ure = upad[..., 0, 1:-1, 1:-1]
    uim = upad[..., 1, 1:-1, 1:-1]
    rre = source[..., 0, :, :] - (dre * ure - dim * uim) + nbr[..., 0, :, :]
    rim = source[..., 1, :, :] - (dre * uim + dim * ure) + nbr[..., 1, :, :]
    new_re = ure + OMEGA * (ire * rre - iim * rim)
    new_im = uim + OMEGA * (ire * rim + iim * rre)
    return jnp.stack([new_re, new_im], axis=-3)

def compress(samples):
    gram = jnp.einsum('bmpk,bmqk->bmpq', samples, samples, precision=lax.Precision.HIGHEST)
    lower_factor = jnp.linalg.cholesky(gram)
    return jax.scipy.linalg.solve_triangular(lower_factor, samples, lower=True)

def reference(probes, slowness, absorbing, partition):
    dre, dim, ire, iim = coefficients(slowness, absorbing)

    def sweep_probe(source):
        field_now = jnp.zeros_like(source)
        for step in range(ITERS):
            padded = jnp.pad(field_now, ((0, 0), (1, 1), (1, 1)))
            field_now = relax(padded, source, dre, dim, ire, iim)
        return field_now
    field = lax.map(sweep_probe, probes)
    traces = jnp.stack([field[:, :, NX // 2 - 1, :], field[:, :, NX // 2, :]])
    index_table = partition.reshape(NB, BS)
    picked = jnp.take(traces, index_table, axis=3)
    samples = jnp.transpose(picked, (3, 0, 1, 2, 4)).reshape(NB, 2, 2 * PROBES, BS)
    return (field, compress(samples))
```

```python
import functools

import jax
import jax.numpy as jnp
from jax import lax
from jax.experimental import pallas as pl
from jax.experimental.pallas import tpu as pltpu
from jax.sharding import PartitionSpec as P

ITERS = 9
BS = 64
OMEGA = 0.8
BETA = 0.5
SIGMA = 1.5

MESH = pl.DeviceIdType.MESH
PLANE = 32
GROUP = 8
PROBES = 16
PAIR = 2
OWN = 2 * GROUP
HALO = 8
ROWS = OWN + 2 * HALO
MAIN = 4
WIDE = 5
F32 = jnp.float32


def lanes():
    return lax.broadcasted_iota(jnp.int32, (8, 128), 1)


def sublanes():
    return lax.broadcasted_iota(jnp.int32, (8, 128), 0)


def widen(tiles, left, right):
    low = lanes() < 64
    sub = sublanes()
    turned = [pltpu.roll(t, 64, 1) for t in tiles]
    left, right = pltpu.roll(left, 64, 1), pltpu.roll(right, 64, 1)
    before = jnp.where(sub == 0, left, pltpu.roll(turned[3], 1, 0))
    after = jnp.where(sub == 7, right, pltpu.roll(turned[0], 7, 0))
    ends = [before] + turned + [after]
    return [jnp.where(low, ends[t], ends[t + 1]) for t in range(WIDE)]


def narrow(wide):
    low = lanes() < 64
    turned = [pltpu.roll(t, 64, 1) for t in wide]
    return [jnp.where(low, turned[t], turned[t + 1]) for t in range(MAIN)]


def beside(row):
    lane = lanes()
    ahead = [pltpu.roll(t, 1, 1) for t in row]
    back = [pltpu.roll(t, 127, 1) for t in row]
    out = []
    for t in range(WIDE):
        left = jnp.where(lane == 0, ahead[t - 1], ahead[t]) if t else ahead[t]
        right = jnp.where(lane == 127, back[t + 1], back[t]) if t < WIDE - 1 else back[t]
        out.append(left + right)
    return out


def kernel(
    probes, slow, absorb, partition,
    field, bases,
    inbuf, slowbuf, flags, esend, erecv, sendf, ssend, fbuf, sbuf, coef, gbuf, ubuf, obuf, rbuf, outbuf,
    points, tbuf, picked, gat, mats, based,
    in_sem, es, er, own_sem, fs, fr, zs, zr, rs, rr, out_sem,
    ts, tr, town, gs, gr, gown, base_sem,
):
    layer = lax.axis_index("layer")
    strip = lax.axis_index("strip")
    z = layer // GROUP
    me = lax.rem(layer, GROUP)

    def peer_of(j):
        return lax.rem(me + j, GROUP)

    def from_of(j):
        return lax.rem(me + GROUP - j, GROUP)

    def member(m):
        return (z * GROUP + m, strip)

    place = me * 4 + strip

    def in_plane(d):
        return (z * GROUP + d // 4, lax.rem(d, 4))

    up_id = (layer - GROUP, strip)
    down_id = (layer + GROUP, strip)

    copies = [
        pltpu.make_async_copy(probes, inbuf, in_sem.at[0]),
        pltpu.make_async_copy(slow, slowbuf, in_sem.at[1]),
        pltpu.make_async_copy(absorb, flags, in_sem.at[2]),
        pltpu.make_async_copy(partition.at[pl.ds(16 * z, 16)], points, in_sem.at[3]),
    ]
    for c in copies:
        c.start()

    barrier = pltpu.get_barrier_semaphore()
    for j in range(1, PLANE):
        pl.semaphore_signal(barrier, inc=1, device_id=in_plane(lax.rem(place + j, PLANE)), device_id_type=MESH)

    def meets(other):
        return (z == 3) | (z == 4) | (other == 3) | (other == 4) | (other == z + 1) | (other == z - 1)

    greeted = PLANE - 1
    for dz in range(1, 8):
        other = lax.rem(z + dz, 8)
        greeted = greeted + jnp.where(meets(other), 1, 0)

        @pl.when(meets(other))
        def _():
            pl.semaphore_signal(barrier, inc=1, device_id=(other * GROUP + me, strip), device_id_type=MESH)

    @pl.when(strip == 0)
    def _():
        erecv[0] = jnp.zeros_like(erecv[0])

    @pl.when(strip == 3)
    def _():
        erecv[1] = jnp.zeros_like(erecv[1])

    @pl.when(z == 0)
    def _():
        for p in range(PAIR):
            fbuf[p, 0:HALO] = jnp.zeros((HALO, 2, MAIN, 8, 128), F32)
        sbuf[0:HALO] = jnp.zeros((HALO, 6, 8, 128), F32)

    @pl.when(z == 7)
    def _():
        for p in range(PAIR):
            fbuf[p, HALO + OWN : ROWS] = jnp.zeros((HALO, 2, MAIN, 8, 128), F32)
        sbuf[HALO + OWN : ROWS] = jnp.zeros((HALO, 6, 8, 128), F32)

    for c in copies:
        c.wait()

    for side, chunk in ((0, 0), (1, 31)):
        for r in range(2):
            at = 2 * chunk + r
            for q in range(4):
                esend[side, r, 8 * q : 8 * q + 8, :] = inbuf[pl.ds(512 * q + at, 8, stride=64), :]
            esend[side, r, 32:40, :] = jnp.broadcast_to(slowbuf[at : at + 1, :], (8, 128))

    pl.semaphore_wait(barrier, greeted)

    def edge_copy(side, to):
        return pltpu.make_async_remote_copy(
            src_ref=esend.at[side], dst_ref=erecv.at[1 - side], send_sem=es.at[side], recv_sem=er.at[1 - side],
            device_id=(layer, to), device_id_type=MESH,
        )

    @pl.when(strip > 0)
    def _():
        edge_copy(0, strip - 1).start()

    @pl.when(strip < 3)
    def _():
        edge_copy(1, strip + 1).start()

    def rows_of(m):
        return pl.ds(HALO + 2 * m, 2)

    def f_copy(p, j, dst_member, to):
        return pltpu.make_async_remote_copy(
            src_ref=sendf.at[p, to], dst_ref=fbuf.at[p, rows_of(dst_member)], send_sem=fs.at[p, j], recv_sem=fr.at[p, j],
            device_id=member(to), device_id_type=MESH,
        )

    def s_copy(j, dst_member, to):
        return pltpu.make_async_remote_copy(
            src_ref=ssend.at[to], dst_ref=sbuf.at[rows_of(dst_member)], send_sem=fs.at[2, j], recv_sem=fr.at[2, j],
            device_id=member(to), device_id_type=MESH,
        )

    def own_f(p):
        return pltpu.make_async_copy(sendf.at[p, me], fbuf.at[p, rows_of(me)], own_sem.at[p])

    own_s = pltpu.make_async_copy(ssend.at[me], sbuf.at[rows_of(me)], own_sem.at[2])

    def stage_f(p):
        for m in range(GROUP):
            for r in range(2):
                for c in range(2):
                    for t in range(MAIN):
                        base = ((2 * m + p) * 2 + c) * 64 + 2 * t + r
                        sendf[p, m, r, c, t] = inbuf[pl.ds(base, 8, stride=8), :]

    def stage_s():
        sub = sublanes()
        for r in range(2):
            flag = jnp.full((8, 128), flags[r], jnp.int32).astype(F32)
            tiles = [slowbuf[pl.ds(2 * t + r, 8, stride=8), :] for t in range(MAIN)]
            for m in range(GROUP):
                for t in range(MAIN):
                    ssend[m, r, t] = tiles[t]
                for side in range(2):
                    mine = erecv[side, r, 4 * m : 4 * m + 8, :]
                    there = erecv[side, r, 32:40, :]
                    ssend[m, r, MAIN + side] = jnp.where(sub < 4, mine, jnp.where(sub == 4, there, flag))

    def send_f(p):
        stage_f(p)
        for j in range(1, GROUP):
            f_copy(p, j, me, peer_of(j)).start()
        own_f(p).start()

    send_f(0)

    @pl.when(strip > 0)
    def _():
        edge_copy(0, strip - 1).wait_send()

    @pl.when(strip > 0)
    def _():
        edge_copy(1, strip - 1).wait_recv()

    @pl.when(strip < 3)
    def _():
        edge_copy(1, strip + 1).wait_send()
        edge_copy(0, strip + 1).wait_recv()

    stage_s()
    for j in range(1, GROUP):
        s_copy(j, me, peer_of(j)).start()
    own_s.start()
    send_f(1)

    def forward_ref(k, rows):
        return sbuf.at[rows] if k == 2 else fbuf.at[k, rows]

    def up_copy(k, j, m):
        return pltpu.make_async_remote_copy(
            src_ref=forward_ref(k, rows_of(m)), dst_ref=forward_ref(k, pl.ds(HALO + OWN + 2 * m, 2)),
            send_sem=zs.at[k, j], recv_sem=zr.at[k, j], device_id=up_id, device_id_type=MESH,
        )

    def down_copy(k, j, m):
        return pltpu.make_async_remote_copy(
            src_ref=forward_ref(k, rows_of(m)), dst_ref=forward_ref(k, pl.ds(2 * (m - 4), 2)),
            send_sem=zs.at[k, j], recv_sem=zr.at[k, j], device_id=down_id, device_id_type=MESH,
        )

    def arrive(k, j):
        m = from_of(j)
        if j == 0:
            (own_s if k == 2 else own_f(k)).wait()
        elif k == 2:
            s_copy(j, m, peer_of(j)).wait_recv()
        else:
            f_copy(k, j, m, peer_of(j)).wait_recv()

        @pl.when((m < 4) & (z > 0))
        def _():
            up_copy(k, j, m).start()

        @pl.when((m >= 4) & (z < 7))
        def _():
            down_copy(k, j, m).start()

    def halo_wait(k):
        for j in range(GROUP):
            m = from_of(j)

            @pl.when((m < 4) & (z < 7))
            def _():
                up_copy(k, j, m).wait_recv()

            @pl.when((m >= 4) & (z > 0))
            def _():
                down_copy(k, j, m).wait_recv()

    for j in range(GROUP):
        arrive(0, j)
    for j in range(GROUP):
        arrive(2, j)
    halo_wait(2)

    def coef_row(r, carry):
        tiles = [sbuf[r, t] for t in range(MAIN)]
        left, right = sbuf[r, MAIN], sbuf[r, MAIN + 1]
        flag = jnp.broadcast_to(left[5:6, :], (8, 128))
        wide = widen(tiles, jnp.broadcast_to(left[4:5, :], (8, 128)), jnp.broadcast_to(right[4:5, :], (8, 128)))
        lane, sub = lanes(), sublanes()
        inside = ((r >= HALO) | (z > 0)) & ((r < HALO + OWN) | (z < 7))
        for t in range(WIDE):
            dre = 4.0 - wide[t]
            dim = BETA * wide[t] + SIGMA * flag
            scale = OMEGA / (dre * dre + dim * dim)
            keep = jnp.full((8, 128), inside)
            if t == 0:
                keep = keep & ((lane >= 64) | (sub > 0) | jnp.full((8, 128), strip > 0))
            if t == WIDE - 1:
                keep = keep & ((lane < 64) | (sub < 7) | jnp.full((8, 128), strip < 3))
            coef[r, 0, t] = jnp.where(keep, dre * scale, 0.0)
            coef[r, 1, t] = jnp.where(keep, -dim * scale, 0.0)
        return carry

    lax.fori_loop(0, ROWS, coef_row, 0)
    halo_wait(0)

    def source_row(p):
        def body(r, carry):
            left, right = sbuf[r, MAIN], sbuf[r, MAIN + 1]
            wide = []
            for c in range(2):
                at = 2 * p + c
                wide.append(
                    widen(
                        [fbuf[p, r, c, t] for t in range(MAIN)],
                        jnp.broadcast_to(left[at : at + 1, :], (8, 128)),
                        jnp.broadcast_to(right[at : at + 1, :], (8, 128)),
                    )
                )
            for t in range(WIDE):
                er_, ei_ = coef[r, 0, t], coef[r, 1, t]
                fr_, fi_ = wide[0][t], wide[1][t]
                gbuf[p, r, 0, t] = er_ * fr_ - ei_ * fi_
                gbuf[p, r, 1, t] = er_ * fi_ + ei_ * fr_
            return carry

        lax.fori_loop(0, ROWS, body, 0)

    def relaxed(p, r, above, here, below):
        near = beside(here[:WIDE]) + beside(here[WIDE:])
        re, im = [], []
        for t in range(WIDE):
            er_, ei_ = coef[r, 0, t], coef[r, 1, t]
            nr = above[t] + below[t] + near[t]
            ni = above[WIDE + t] + below[WIDE + t] + near[WIDE + t]
            re.append((1.0 - OMEGA) * here[t] + gbuf[p, r, 0, t] + (er_ * nr - ei_ * ni))
            im.append((1.0 - OMEGA) * here[WIDE + t] + gbuf[p, r, 1, t] + (er_ * ni + ei_ * nr))
        return re + im

    def load(ref, p, r):
        return [ref[p, r, c, t] for c in range(2) for t in range(WIDE)]

    def store(p, r, row):
        for c in range(2):
            for t in range(WIDE):
                ubuf[p, r, c, t] = row[c * WIDE + t]

    def sweep(p, step):
        src = gbuf if step == 2 else ubuf
        low, high = step - 1, ROWS + 1 - step

        def body(i, carry):
            r = low + 2 * i
            above, here = carry[: 2 * WIDE], carry[2 * WIDE :]
            below = load(src, p, r + 1)
            new = relaxed(p, r, above, here, below)
            after = load(src, p, r + 2)
            if step < ITERS:
                store(p, r, new)
            new2 = relaxed(p, r + 1, here, below, after)
            if step < ITERS:
                store(p, r + 1, new2)
            else:
                for rr_, row in ((r, new), (r + 1, new2)):
                    for c in range(2):
                        tiles = narrow(row[c * WIDE : (c + 1) * WIDE])
                        for t in range(MAIN):
                            obuf[p, rr_ - HALO, c, t] = tiles[t]
            return tuple(below) + tuple(after)

        lax.fori_loop(0, (high - low) // 2, body, tuple(load(src, p, low - 1)) + tuple(load(src, p, low)))

    def back_copy(p, j, of_member, to):
        return pltpu.make_async_remote_copy(
            src_ref=obuf.at[p, pl.ds(2 * to, 2)], dst_ref=rbuf.at[2 * of_member + p], send_sem=rs.at[p, j], recv_sem=rr.at[p, j],
            device_id=member(to), device_id_type=MESH,
        )

    def own_back(p):
        return pltpu.make_async_copy(obuf.at[p, pl.ds(2 * me, 2)], rbuf.at[2 * me + p], own_sem.at[3 + p])

    def send_back(p):
        for j in range(1, GROUP):
            back_copy(p, j, me, peer_of(j)).start()
        own_back(p).start()

    def out_copy(p, j):
        at = pl.ds((2 * from_of(j) + p) * 128, 128)
        return pltpu.make_async_copy(outbuf.at[at], field.at[at], out_sem.at[p, j])

    def receive_back(p):
        for j in range(GROUP):
            m = from_of(j)
            if j == 0:
                own_back(p).wait()
            else:
                back_copy(p, j, m, peer_of(j)).wait_recv()
            q = 2 * m + p
            for r in range(2):
                for c in range(2):
                    for t in range(MAIN):
                        outbuf[pl.ds((q * 2 + c) * 64 + 2 * t + r, 8, stride=8), :] = rbuf[q, r, c, t]
            out_copy(p, j).start()

    def trace_copy(side, p, other):
        return pltpu.make_async_remote_copy(
            src_ref=obuf.at[p, OWN - 1 if side == 0 else 0], dst_ref=tbuf.at[side, p],
            send_sem=ts.at[p, other], recv_sem=tr.at[side, p],
            device_id=(other * GROUP + me, strip), device_id_type=MESH,
        )

    def trace_own(side, p):
        return pltpu.make_async_copy(obuf.at[p, OWN - 1 if side == 0 else 0], tbuf.at[side, p], town.at[p])

    def trace_send(p):
        for side in range(2):
            owner = 3 + side

            @pl.when(z == owner)
            def _():
                for other in range(8):
                    if other == owner:
                        trace_own(side, p).start()
                    else:
                        trace_copy(side, p, other).start()

    def trace_wait(p):
        for side in range(2):
            owner = 3 + side

            @pl.when(z == owner)
            def _():
                trace_own(side, p).wait()

            @pl.when(z != owner)
            def _():
                trace_copy(side, p, 0).wait_recv()

    def pick(g, carry):
        sub = sublanes()
        at = jnp.broadcast_to(points[pl.ds(g, 1), :], (8, 128)) - strip * 4096
        tile, lane = (at >> 7) & 3, at & 127
        hit = (at >> 9) == sub
        rows = jnp.zeros((8, 128), F32)
        for side in range(2):
            for p in range(PAIR):
                for c in range(2):
                    got = [jnp.take_along_axis(tbuf[side, p, c, t], lane, axis=1) for t in range(MAIN)]
                    best = got[0]
                    for t in range(1, MAIN):
                        best = jnp.where(tile == t, got[t], best)
                    one = jnp.sum(jnp.where(hit, best, 0.0), axis=0, keepdims=True)
                    rows = jnp.where(sub == side * 4 + p * 2 + c, jnp.broadcast_to(one, (8, 128)), rows)
        picked[g] = rows
        return carry

    def picked_copy(j, source, to):
        return pltpu.make_async_remote_copy(
            src_ref=picked.at[to // 2], dst_ref=gat.at[source], send_sem=gs.at[j], recv_sem=gr.at[j],
            device_id=in_plane(to), device_id_type=MESH,
        )

    picked_own = pltpu.make_async_copy(picked.at[place // 2], gat.at[place], gown)

    def pick_send():
        lax.fori_loop(0, 16, pick, 0)
        for j in range(1, PLANE):
            picked_copy(j, place, lax.rem(place + j, PLANE)).start()
        picked_own.start()

    def compress():
        for j in range(1, PLANE):
            picked_copy(j, lax.rem(place + PLANE - j, PLANE), lax.rem(place + j, PLANE)).wait_recv()
        picked_own.wait()
        lane32 = lax.broadcasted_iota(jnp.int32, (32, 128), 1)
        row32 = lax.broadcasted_iota(jnp.int32, (32, 128), 0)
        odd = jnp.full((8, 128), lax.rem(strip, 2) == 1)
        for m in range(GROUP):
            tile = (gat[4 * m] + gat[4 * m + 1]) + (gat[4 * m + 2] + gat[4 * m + 3])
            tile = jnp.where(odd, pltpu.roll(tile, 64, 1), tile)
            tile = jnp.where(lanes() < 64, tile, 0.0)
            for side in range(2):
                mats[side, 4 * m : 4 * m + 4, :] = tile[4 * side : 4 * side + 4, :]
        augmented = []
        for side in range(2):
            mat = mats[side]
            zero = jnp.zeros((32, 128), F32)
            spread = jnp.concatenate([zero, zero, mat, zero], axis=0)
            gram = lax.dot_general(
                mat, spread, (((1,), (1,)), ((), ())), precision=lax.Precision.HIGHEST, preferred_element_type=F32
            )
            augmented.append(jnp.where(lane32 < 64, mat, gram))
        for k in range(32):
            for side in range(2):
                a = augmented[side]
                inverse = lax.rsqrt(a[k : k + 1, 64 + k : 65 + k])
                row = a[k : k + 1, :] * inverse
                column = a[:, 64 + k : 65 + k] * inverse
                less = a - column * row
                augmented[side] = jnp.where(row32 > k, less, jnp.where(row32 == k, jnp.broadcast_to(row, (32, 128)), a))
        for side in range(2):
            based[side] = augmented[side][:, :BS]
        pltpu.make_async_copy(based, bases, base_sem).start()

    source_row(0)
    for step in range(2, ITERS + 1):
        sweep(0, step)
        arrive(1, step - 2)
    trace_send(0)
    send_back(0)
    halo_wait(1)
    source_row(1)
    for step in range(2, ITERS + 1):
        sweep(1, step)
    trace_send(1)
    send_back(1)
    trace_wait(0)
    receive_back(0)
    trace_wait(1)
    pick_send()
    compress()
    receive_back(1)

    for j in range(1, GROUP):
        for p in range(PAIR):
            f_copy(p, j, me, peer_of(j)).wait_send()
            back_copy(p, j, me, peer_of(j)).wait_send()
        s_copy(j, me, peer_of(j)).wait_send()
    for k in range(3):
        for j in range(GROUP):
            m = from_of(j)

            @pl.when((m < 4) & (z > 0))
            def _():
                up_copy(k, j, m).wait_send()

            @pl.when((m >= 4) & (z < 7))
            def _():
                down_copy(k, j, m).wait_send()

    for p in range(PAIR):
        for side in range(2):

            @pl.when(z == 3 + side)
            def _():
                for other in range(8):
                    if other != 3 + side:
                        trace_copy(side, p, other).wait_send()

    for j in range(1, PLANE):
        picked_copy(j, place, lax.rem(place + j, PLANE)).wait_send()
    for p in range(PAIR):
        for j in range(GROUP):
            out_copy(p, j).wait()
    pltpu.make_async_copy(based, bases, base_sem).wait()


def swept(probes, slow, absorb, partition):
    any_space = pl.BlockSpec(memory_space=pl.ANY)
    dma = pltpu.SemaphoreType.DMA
    return pl.pallas_call(
        kernel,
        out_shape=(
            jax.ShapeDtypeStruct((2 * PROBES * 64, 128), F32),
            jax.ShapeDtypeStruct((2, 2 * PROBES, BS), F32),
        ),
        in_specs=[any_space] * 4,
        out_specs=(any_space, any_space),
        scratch_shapes=[
            pltpu.VMEM((2 * PROBES * 64, 128), F32),
            pltpu.VMEM((64, 128), F32),
            pltpu.SMEM((2,), jnp.int32),
            pltpu.VMEM((2, 2, 40, 128), F32),
            pltpu.VMEM((2, 2, 40, 128), F32),
            pltpu.VMEM((PAIR, GROUP, 2, 2, MAIN, 8, 128), F32),
            pltpu.VMEM((GROUP, 2, 6, 8, 128), F32),
            pltpu.VMEM((PAIR, ROWS, 2, MAIN, 8, 128), F32),
            pltpu.VMEM((ROWS, 6, 8, 128), F32),
            pltpu.VMEM((ROWS, 2, WIDE, 8, 128), F32),
            pltpu.VMEM((PAIR, ROWS, 2, WIDE, 8, 128), F32),
            pltpu.VMEM((PAIR, ROWS, 2, WIDE, 8, 128), F32),
            pltpu.VMEM((PAIR, OWN, 2, MAIN, 8, 128), F32),
            pltpu.VMEM((PROBES, 2, 2, MAIN, 8, 128), F32),
            pltpu.VMEM((2 * PROBES * 64, 128), F32),
            pltpu.VMEM((16, 128), jnp.int32),
            pltpu.VMEM((2, PAIR, 2, MAIN, 8, 128), F32),
            pltpu.VMEM((16, 8, 128), F32),
            pltpu.VMEM((PLANE, 8, 128), F32),
            pltpu.VMEM((2, 32, 128), F32),
            pltpu.VMEM((2, 32, BS), F32),
            dma((4,)),
            dma((2,)),
            dma((2,)),
            dma((5,)),
            dma((3, GROUP)),
            dma((3, GROUP)),
            dma((3, GROUP)),
            dma((3, GROUP)),
            dma((PAIR, GROUP)),
            dma((PAIR, GROUP)),
            dma((PAIR, GROUP)),
            dma((PAIR, 8)),
            dma((2, PAIR)),
            dma((PAIR,)),
            dma((PLANE,)),
            dma((PLANE,)),
            dma(()),
            dma(()),
        ],
        compiler_params=pltpu.CompilerParams(
            collective_id=1, has_side_effects=True, vmem_limit_bytes=48 * 1024 * 1024
        ),
        name="sweeps",
    )(probes, slow, absorb, partition)


def per_device(probes, slowness, absorbing, partition):
    flat = probes.reshape(PROBES, 2, 2, 32, 128).transpose(0, 1, 3, 2, 4).reshape(2 * PROBES * 64, 128)
    slow = slowness.reshape(2, 32, 128).transpose(1, 0, 2).reshape(64, 128)
    out, bases = swept(flat, slow, absorbing, partition.reshape(128, 128))
    field = out.reshape(PROBES, 2, 32, 2, 128).transpose(0, 1, 3, 2, 4).reshape(PROBES, 2, 2, 4096)
    return field, bases[None]


def solution(mesh):
    return jax.shard_map(
        per_device,
        mesh=mesh,
        in_specs=(P(None, None, "layer", "strip"), P("layer", "strip"), P("layer"), P()),
        out_specs=(P(None, None, "layer", "strip"), P(("layer", "strip"), None, None, None)),
        check_vma=False,
    )
```

```python
import functools

import jax
import jax.numpy as jnp
from jax import lax
from jax.experimental import pallas as pl
from jax.experimental.pallas import tpu as pltpu
from jax.sharding import PartitionSpec as P

ITERS = 9
BS = 64
BLOCK = 8
OMEGA = 0.8
BETA = 0.5
SIGMA = 1.5

MESH = pl.DeviceIdType.MESH
PLANE = 32
GROUP = 8
PROBES = 16
PAIR = 2
OWN = 2 * GROUP
HALO = 8
ROWS = OWN + 2 * HALO
MAIN = 4
WIDE = 5
F32 = jnp.float32
VMEM_LIMIT = 62 * 1024 * 1024


def lanes():
    return lax.broadcasted_iota(jnp.int32, (8, 128), 1)


def sublanes():
    return lax.broadcasted_iota(jnp.int32, (8, 128), 0)


def widen(tiles, left, right):
    low = lanes() < 64
    sub = sublanes()
    turned = [pltpu.roll(t, 64, 1) for t in tiles]
    left, right = pltpu.roll(left, 64, 1), pltpu.roll(right, 64, 1)
    before = jnp.where(sub == 0, left, pltpu.roll(turned[3], 1, 0))
    after = jnp.where(sub == 7, right, pltpu.roll(turned[0], 7, 0))
    ends = [before] + turned + [after]
    return [jnp.where(low, ends[t], ends[t + 1]) for t in range(WIDE)]


def narrow(wide):
    low = lanes() < 64
    turned = [pltpu.roll(t, 64, 1) for t in wide]
    return [jnp.where(low, turned[t], turned[t + 1]) for t in range(MAIN)]


def beside(row):
    lane = lanes()
    ahead = [pltpu.roll(t, 1, 1) for t in row]
    back = [pltpu.roll(t, 127, 1) for t in row]
    out = []
    for t in range(WIDE):
        left = jnp.where(lane == 0, ahead[t - 1], ahead[t]) if t else ahead[t]
        right = jnp.where(lane == 127, back[t + 1], back[t]) if t < WIDE - 1 else back[t]
        out.append(left + right)
    return out


def kernel(
    probes, slow, absorb, partition,
    field, bases,
    inbuf, slowbuf, flags, esend, erecv, sendf, ssend, epack, fbuf, sbuf, ebuf, coef, gbuf, ubuf, vbuf, obuf, rbuf,
    points, tbuf, picked, gat, mats,
    in_sem, es, er, own_sem, fs, fr, zs, zr, rs, rr,
    ts, tr, town, gs, gr, gown,
):
    layer = lax.axis_index("layer")
    strip = lax.axis_index("strip")
    z = layer // GROUP
    me = lax.rem(layer, GROUP)

    def peer_of(j):
        return lax.rem(me + j, GROUP)

    def from_of(j):
        return lax.rem(me + GROUP - j, GROUP)

    def member(m):
        return (z * GROUP + m, strip)

    place = me * 4 + strip

    def in_plane(d):
        return (z * GROUP + d // 4, lax.rem(d, 4))

    up_id = (layer - GROUP, strip)
    down_id = (layer + GROUP, strip)

    copies = [
        pltpu.make_async_copy(probes, inbuf, in_sem.at[0]),
        pltpu.make_async_copy(slow, slowbuf, in_sem.at[1]),
        pltpu.make_async_copy(absorb, flags, in_sem.at[2]),
        pltpu.make_async_copy(partition.at[pl.ds(16 * z, 16)], points, in_sem.at[3]),
    ]
    for c in copies:
        c.start()

    barrier = pltpu.get_barrier_semaphore()
    for j in range(1, PLANE):
        pl.semaphore_signal(barrier, inc=1, device_id=in_plane(lax.rem(place + j, PLANE)), device_id_type=MESH)

    def meets(other):
        return (z == 3) | (z == 4) | (other == 3) | (other == 4) | (other == z + 1) | (other == z - 1)

    greeted = PLANE - 1
    for dz in range(1, 8):
        other = lax.rem(z + dz, 8)
        greeted = greeted + jnp.where(meets(other), 1, 0)

        @pl.when(meets(other))
        def _():
            pl.semaphore_signal(barrier, inc=1, device_id=(other * GROUP + me, strip), device_id_type=MESH)

    @pl.when(strip == 0)
    def _():
        erecv[0] = jnp.zeros_like(erecv[0])

    @pl.when(strip == 3)
    def _():
        erecv[1] = jnp.zeros_like(erecv[1])

    @pl.when(z == 0)
    def _():
        for p in range(PAIR):
            fbuf[p, 0:HALO] = jnp.zeros((HALO, 2, MAIN, 8, 128), F32)
        sbuf[0:HALO] = jnp.zeros((HALO, MAIN, 8, 128), F32)
        ebuf[0:HALO] = jnp.zeros((HALO, 2, 8, 128), F32)

    @pl.when(z == 7)
    def _():
        for p in range(PAIR):
            fbuf[p, HALO + OWN : ROWS] = jnp.zeros((HALO, 2, MAIN, 8, 128), F32)
        sbuf[HALO + OWN : ROWS] = jnp.zeros((HALO, MAIN, 8, 128), F32)
        ebuf[HALO + OWN : ROWS] = jnp.zeros((HALO, 2, 8, 128), F32)

    for c in copies:
        c.wait()

    for side, chunk in ((0, 0), (1, 31)):
        for r in range(2):
            at = 2 * chunk + r
            for q in range(4):
                esend[side, r, 8 * q : 8 * q + 8, :] = inbuf[pl.ds(512 * q + at, 8, stride=64), :]
            esend[side, r, 32:40, :] = jnp.broadcast_to(slowbuf[at : at + 1, :], (8, 128))

    pl.semaphore_wait(barrier, greeted)

    def edge_copy(side, to):
        return pltpu.make_async_remote_copy(
            src_ref=esend.at[side], dst_ref=erecv.at[1 - side], send_sem=es.at[side], recv_sem=er.at[1 - side],
            device_id=(layer, to), device_id_type=MESH,
        )

    @pl.when(strip > 0)
    def _():
        edge_copy(0, strip - 1).start()

    @pl.when(strip < 3)
    def _():
        edge_copy(1, strip + 1).start()

    def rows_of(m):
        return pl.ds(HALO + 2 * m, 2)

    def f_copy(p, j, dst_member, to):
        return pltpu.make_async_remote_copy(
            src_ref=sendf.at[p, to], dst_ref=fbuf.at[p, rows_of(dst_member)], send_sem=fs.at[p, j], recv_sem=fr.at[p, j],
            device_id=member(to), device_id_type=MESH,
        )

    def s_copy(j, dst_member, to):
        return pltpu.make_async_remote_copy(
            src_ref=ssend, dst_ref=sbuf.at[rows_of(dst_member)], send_sem=fs.at[2, j], recv_sem=fr.at[2, j],
            device_id=member(to), device_id_type=MESH,
        )

    def e_copy(j, dst_member, to):
        return pltpu.make_async_remote_copy(
            src_ref=epack.at[to], dst_ref=ebuf.at[rows_of(dst_member)], send_sem=fs.at[3, j], recv_sem=fr.at[3, j],
            device_id=member(to), device_id_type=MESH,
        )

    def own_f(p):
        return pltpu.make_async_copy(sendf.at[p, me], fbuf.at[p, rows_of(me)], own_sem.at[p])

    own_s = pltpu.make_async_copy(ssend, sbuf.at[rows_of(me)], own_sem.at[2])
    own_e = pltpu.make_async_copy(epack.at[me], ebuf.at[rows_of(me)], own_sem.at[5])

    def stage_f(p):
        for m in range(GROUP):
            for r in range(2):
                for c in range(2):
                    for t in range(MAIN):
                        base = ((2 * m + p) * 2 + c) * 64 + 2 * t + r
                        sendf[p, m, r, c, t] = inbuf[pl.ds(base, 8, stride=8), :]

    def stage_s():
        for r in range(2):
            for t in range(MAIN):
                ssend[r, t] = slowbuf[pl.ds(2 * t + r, 8, stride=8), :]

    def stage_e():
        sub = sublanes()
        for r in range(2):
            flag = jnp.full((8, 128), flags[r], jnp.int32).astype(F32)
            for m in range(GROUP):
                for side in range(2):
                    mine = erecv[side, r, 4 * m : 4 * m + 8, :]
                    there = erecv[side, r, 32:40, :]
                    epack[m, r, side] = jnp.where(sub < 4, mine, jnp.where(sub == 4, there, flag))

    def send_f(p):
        stage_f(p)
        for j in range(1, GROUP):
            f_copy(p, j, me, peer_of(j)).start()
        own_f(p).start()

    send_f(0)
    stage_s()
    for j in range(1, GROUP):
        s_copy(j, me, peer_of(j)).start()
    own_s.start()

    @pl.when(strip > 0)
    def _():
        edge_copy(0, strip - 1).wait_send()
        edge_copy(1, strip - 1).wait_recv()

    @pl.when(strip < 3)
    def _():
        edge_copy(1, strip + 1).wait_send()
        edge_copy(0, strip + 1).wait_recv()

    stage_e()
    for j in range(1, GROUP):
        e_copy(j, me, peer_of(j)).start()
    own_e.start()

    def forward_ref(k, rows):
        return (ebuf if k == 3 else sbuf).at[rows] if k >= 2 else fbuf.at[k, rows]

    def up_copy(k, j, m):
        return pltpu.make_async_remote_copy(
            src_ref=forward_ref(k, rows_of(m)), dst_ref=forward_ref(k, pl.ds(HALO + OWN + 2 * m, 2)),
            send_sem=zs.at[k, j], recv_sem=zr.at[k, j], device_id=up_id, device_id_type=MESH,
        )

    def down_copy(k, j, m):
        return pltpu.make_async_remote_copy(
            src_ref=forward_ref(k, rows_of(m)), dst_ref=forward_ref(k, pl.ds(2 * (m - 4), 2)),
            send_sem=zs.at[k, j], recv_sem=zr.at[k, j], device_id=down_id, device_id_type=MESH,
        )

    def arrive(k, j):
        m = from_of(j)
        if j == 0:
            (own_e if k == 3 else own_s if k == 2 else own_f(k)).wait()
        elif k == 2:
            s_copy(j, m, peer_of(j)).wait_recv()
        elif k == 3:
            e_copy(j, m, peer_of(j)).wait_recv()
        else:
            f_copy(k, j, m, peer_of(j)).wait_recv()

        @pl.when((m < 4) & (z > 0))
        def _():
            up_copy(k, j, m).start()

        @pl.when((m >= 4) & (z < 7))
        def _():
            down_copy(k, j, m).start()

    def halo_wait(k):
        for j in range(GROUP):
            m = from_of(j)

            @pl.when((m < 4) & (z < 7))
            def _():
                up_copy(k, j, m).wait_recv()

            @pl.when((m >= 4) & (z > 0))
            def _():
                down_copy(k, j, m).wait_recv()

    for j in range(GROUP):
        arrive(0, j)
    for j in range(GROUP):
        arrive(2, j)
    send_f(1)
    for j in range(GROUP):
        arrive(3, j)
    halo_wait(2)
    halo_wait(3)

    def by_rows(work):
        def four(i, carry):
            for n in range(4):
                work(4 * i + n)
            return carry

        lax.fori_loop(0, ROWS // 4, four, 0)

    def coef_row(r):
        tiles = [sbuf[r, t] for t in range(MAIN)]
        left, right = ebuf[r, 0], ebuf[r, 1]
        flag = jnp.broadcast_to(left[5:6, :], (8, 128))
        wide = widen(tiles, jnp.broadcast_to(left[4:5, :], (8, 128)), jnp.broadcast_to(right[4:5, :], (8, 128)))
        lane, sub = lanes(), sublanes()
        inside = ((r >= HALO) | (z > 0)) & ((r < HALO + OWN) | (z < 7))
        for t in range(WIDE):
            dre = 4.0 - wide[t]
            dim = BETA * wide[t] + SIGMA * flag
            scale = OMEGA / (dre * dre + dim * dim)
            keep = jnp.full((8, 128), inside)
            if t == 0:
                keep = keep & ((lane >= 64) | (sub > 0) | jnp.full((8, 128), strip > 0))
            if t == WIDE - 1:
                keep = keep & ((lane < 64) | (sub < 7) | jnp.full((8, 128), strip < 3))
            coef[r, 0, t] = jnp.where(keep, dre * scale, 0.0)
            coef[r, 1, t] = jnp.where(keep, -dim * scale, 0.0)

    by_rows(coef_row)
    halo_wait(0)

    def source_row(p):
        def body(r):
            left, right = ebuf[r, 0], ebuf[r, 1]
            wide = []
            for c in range(2):
                at = 2 * p + c
                wide.append(
                    widen(
                        [fbuf[p, r, c, t] for t in range(MAIN)],
                        jnp.broadcast_to(left[at : at + 1, :], (8, 128)),
                        jnp.broadcast_to(right[at : at + 1, :], (8, 128)),
                    )
                )
            for t in range(WIDE):
                er_, ei_ = coef[r, 0, t], coef[r, 1, t]
                fr_, fi_ = wide[0][t], wide[1][t]
                gbuf[p, r, 0, t] = er_ * fr_ - ei_ * fi_
                gbuf[p, r, 1, t] = er_ * fi_ + ei_ * fr_

        by_rows(body)

    def relaxed(p, r, above, here, below):
        near = beside(here[:WIDE]) + beside(here[WIDE:])
        re, im = [], []
        for t in range(WIDE):
            er_, ei_ = coef[r, 0, t], coef[r, 1, t]
            nr = above[t] + below[t] + near[t]
            ni = above[WIDE + t] + below[WIDE + t] + near[WIDE + t]
            re.append((1.0 - OMEGA) * here[t] + gbuf[p, r, 0, t] + (er_ * nr - ei_ * ni))
            im.append((1.0 - OMEGA) * here[WIDE + t] + gbuf[p, r, 1, t] + (er_ * ni + ei_ * nr))
        return re + im

    def load(ref, p, r):
        return [ref[p, r, c, t] for c in range(2) for t in range(WIDE)]

    def sweep(p, step):
        src = gbuf if step == 2 else (ubuf if step % 2 else vbuf)
        dst = vbuf if step % 2 else ubuf
        low, count = step - 1, ROWS + 2 - 2 * step
        block = {30: 10, 28: 7, 26: 13, 24: 8, 22: 11, 20: 10, 18: 9, 16: 8}[count]

        def body(i, carry):
            above, here = list(carry[: 2 * WIDE]), list(carry[2 * WIDE :])
            for n in range(block):
                r = low + block * i + n
                below = load(src, p, r + 1)
                new = relaxed(p, r, above, here, below)
                if step < ITERS:
                    for c in range(2):
                        for t in range(WIDE):
                            dst[p, r, c, t] = new[c * WIDE + t]
                else:
                    for c in range(2):
                        tiles = narrow(new[c * WIDE : (c + 1) * WIDE])
                        for t in range(MAIN):
                            obuf[p, r - HALO, c, t] = tiles[t]
                above, here = here, below
            return tuple(above) + tuple(here)

        lax.fori_loop(0, count // block, body, tuple(load(src, p, low - 1)) + tuple(load(src, p, low)))

    def back_copy(p, j, of_member, to):
        return pltpu.make_async_remote_copy(
            src_ref=obuf.at[p, pl.ds(2 * to, 2)], dst_ref=rbuf.at[2 * of_member + p], send_sem=rs.at[p, j], recv_sem=rr.at[p, j],
            device_id=member(to), device_id_type=MESH,
        )

    def own_back(p):
        return pltpu.make_async_copy(obuf.at[p, pl.ds(2 * me, 2)], rbuf.at[2 * me + p], own_sem.at[3 + p])

    def send_back(p):
        for j in range(1, GROUP):
            back_copy(p, j, me, peer_of(j)).start()
        own_back(p).start()

    def receive_back(p):
        for j in range(GROUP):
            m = from_of(j)
            if j == 0:
                own_back(p).wait()
            else:
                back_copy(p, j, m, peer_of(j)).wait_recv()
            q = 2 * m + p
            for r in range(2):
                for c in range(2):
                    for t in range(MAIN):
                        field[pl.ds((q * 2 + c) * 64 + 2 * t + r, 8, stride=8), :] = rbuf[q, r, c, t]

    def trace_copy(side, p, other):
        return pltpu.make_async_remote_copy(
            src_ref=obuf.at[p, OWN - 1 if side == 0 else 0], dst_ref=tbuf.at[side, p],
            send_sem=ts.at[p, other], recv_sem=tr.at[side, p],
            device_id=(other * GROUP + me, strip), device_id_type=MESH,
        )

    def trace_own(side, p):
        return pltpu.make_async_copy(obuf.at[p, OWN - 1 if side == 0 else 0], tbuf.at[side, p], town.at[p])

    def trace_send(p):
        for side in range(2):
            owner = 3 + side

            @pl.when(z == owner)
            def _():
                for other in range(8):
                    if other == owner:
                        trace_own(side, p).start()
                    else:
                        trace_copy(side, p, other).start()

    def trace_wait(p):
        for side in range(2):
            owner = 3 + side

            @pl.when(z == owner)
            def _():
                trace_own(side, p).wait()

            @pl.when(z != owner)
            def _():
                trace_copy(side, p, 0).wait_recv()

    def pick(p, g):
        sub = sublanes()
        at = jnp.broadcast_to(points[pl.ds(g, 1), :], (8, 128)) - strip * 4096
        tile, lane = (at >> 7) & 3, at & 127
        hit = (at >> 9) == sub
        rows = jnp.zeros((8, 128), F32) if p == 0 else picked[g]
        for side in range(2):
            for c in range(2):
                got = [jnp.take_along_axis(tbuf[side, p, c, t], lane, axis=1) for t in range(MAIN)]
                best = got[0]
                for t in range(1, MAIN):
                    best = jnp.where(tile == t, got[t], best)
                one = jnp.sum(jnp.where(hit, best, 0.0), axis=0, keepdims=True)
                rows = jnp.where(sub == side * 4 + p * 2 + c, jnp.broadcast_to(one, (8, 128)), rows)
        picked[g] = rows

    def pick_all(p):
        def four(i, carry):
            for n in range(4):
                pick(p, 4 * i + n)
            return carry

        lax.fori_loop(0, 4, four, 0)

    def picked_copy(j, source, to):
        return pltpu.make_async_remote_copy(
            src_ref=picked.at[to // 2], dst_ref=gat.at[source], send_sem=gs.at[j], recv_sem=gr.at[j],
            device_id=in_plane(to), device_id_type=MESH,
        )

    picked_own = pltpu.make_async_copy(picked.at[place // 2], gat.at[place], gown)

    def pick_send():
        pick_all(1)
        for j in range(1, PLANE):
            picked_copy(j, place, lax.rem(place + j, PLANE)).start()
        picked_own.start()

    def compress():
        for j in range(1, PLANE):
            picked_copy(j, lax.rem(place + PLANE - j, PLANE), lax.rem(place + j, PLANE)).wait_recv()
        picked_own.wait()
        lane32 = lax.broadcasted_iota(jnp.int32, (32, 128), 1)
        row32 = lax.broadcasted_iota(jnp.int32, (32, 128), 0)
        odd = jnp.full((8, 128), lax.rem(strip, 2) == 1)
        for m in range(GROUP):
            tile = (gat[4 * m] + gat[4 * m + 1]) + (gat[4 * m + 2] + gat[4 * m + 3])
            tile = jnp.where(odd, pltpu.roll(tile, 64, 1), tile)
            tile = jnp.where(lanes() < 64, tile, 0.0)
            for side in range(2):
                mats[side, 4 * m : 4 * m + 4, :] = tile[4 * side : 4 * side + 4, :]
        augmented = []
        for side in range(2):
            mat = mats[side]
            zero = jnp.zeros((32, 128), F32)
            spread = jnp.concatenate([zero, zero, mat, zero], axis=0)
            gram = lax.dot_general(
                mat, spread, (((1,), (1,)), ((), ())), precision=lax.Precision.HIGHEST, preferred_element_type=F32
            )
            augmented.append(jnp.where(lane32 < 64, mat, gram))
        for first in range(0, 32, BLOCK):
            spread = [
                [jnp.broadcast_to(a[:, 64 + k : 65 + k], (32, 128)) for k in range(first, first + BLOCK)] for a in augmented
            ]
            for j in range(BLOCK):
                k = first + j
                for side in range(2):
                    a, columns = augmented[side], spread[side]
                    inverse = lax.rsqrt(jnp.broadcast_to(columns[j][k : k + 1, :], (32, 128)))
                    row = jnp.broadcast_to(a[k : k + 1, :], (32, 128)) * inverse
                    column = columns[j] * inverse
                    augmented[side] = jnp.where(row32 > k, a - column * row, jnp.where(row32 == k, row, a))
                    for i in range(j + 1, BLOCK):
                        across = jnp.broadcast_to(columns[i][k : k + 1, :], (32, 128)) * inverse
                        columns[i] = columns[i] - column * across
        for side in range(2):
            bases[side] = augmented[side][:, :BS]

    source_row(0)
    for step in range(2, ITERS + 1):
        sweep(0, step)
        if step in (2, 3):
            for j in range(4):
                arrive(1, 4 * (step - 2) + j)
    trace_send(0)
    send_back(0)
    halo_wait(1)
    source_row(1)
    for step in range(2, ITERS + 1):
        sweep(1, step)
    trace_send(1)
    send_back(1)
    trace_wait(0)
    pick_all(0)
    receive_back(0)
    trace_wait(1)
    pick_send()
    compress()
    receive_back(1)

    for j in range(1, GROUP):
        for p in range(PAIR):
            f_copy(p, j, me, peer_of(j)).wait_send()
            back_copy(p, j, me, peer_of(j)).wait_send()
        s_copy(j, me, peer_of(j)).wait_send()
        e_copy(j, me, peer_of(j)).wait_send()
    for k in range(4):
        for j in range(GROUP):
            m = from_of(j)

            @pl.when((m < 4) & (z > 0))
            def _():
                up_copy(k, j, m).wait_send()

            @pl.when((m >= 4) & (z < 7))
            def _():
                down_copy(k, j, m).wait_send()

    for p in range(PAIR):
        for side in range(2):

            @pl.when(z == 3 + side)
            def _():
                for other in range(8):
                    if other != 3 + side:
                        trace_copy(side, p, other).wait_send()

    for j in range(1, PLANE):
        picked_copy(j, place, lax.rem(place + j, PLANE)).wait_send()


def swept(probes, slow, absorb, partition):
    far = pl.BlockSpec(memory_space=pltpu.HBM)
    near = pl.BlockSpec(memory_space=pltpu.VMEM)
    dma = pltpu.SemaphoreType.DMA
    return pl.pallas_call(
        kernel,
        out_shape=(
            jax.ShapeDtypeStruct((2 * PROBES * 64, 128), F32),
            jax.ShapeDtypeStruct((2, 2 * PROBES, BS), F32),
        ),
        in_specs=[far] * 4,
        out_specs=(near, near),
        scratch_shapes=[
            pltpu.VMEM((2 * PROBES * 64, 128), F32),
            pltpu.VMEM((64, 128), F32),
            pltpu.SMEM((2,), jnp.int32),
            pltpu.VMEM((2, 2, 40, 128), F32),
            pltpu.VMEM((2, 2, 40, 128), F32),
            pltpu.VMEM((PAIR, GROUP, 2, 2, MAIN, 8, 128), F32),
            pltpu.VMEM((2, MAIN, 8, 128), F32),
            pltpu.VMEM((GROUP, 2, 2, 8, 128), F32),
            pltpu.VMEM((PAIR, ROWS, 2, MAIN, 8, 128), F32),
            pltpu.VMEM((ROWS, MAIN, 8, 128), F32),
            pltpu.VMEM((ROWS, 2, 8, 128), F32),
            pltpu.VMEM((ROWS, 2, WIDE, 8, 128), F32),
            pltpu.VMEM((PAIR, ROWS, 2, WIDE, 8, 128), F32),
            pltpu.VMEM((PAIR, ROWS, 2, WIDE, 8, 128), F32),
            pltpu.VMEM((PAIR, ROWS, 2, WIDE, 8, 128), F32),
            pltpu.VMEM((PAIR, OWN, 2, MAIN, 8, 128), F32),
            pltpu.VMEM((PROBES, 2, 2, MAIN, 8, 128), F32),
            pltpu.VMEM((16, 128), jnp.int32),
            pltpu.VMEM((2, PAIR, 2, MAIN, 8, 128), F32),
            pltpu.VMEM((16, 8, 128), F32),
            pltpu.VMEM((PLANE, 8, 128), F32),
            pltpu.VMEM((2, 32, 128), F32),
            dma((4,)),
            dma((2,)),
            dma((2,)),
            dma((6,)),
            dma((4, GROUP)),
            dma((4, GROUP)),
            dma((4, GROUP)),
            dma((4, GROUP)),
            dma((PAIR, GROUP)),
            dma((PAIR, GROUP)),
            dma((PAIR, 8)),
            dma((2, PAIR)),
            dma((PAIR,)),
            dma((PLANE,)),
            dma((PLANE,)),
            dma(()),
        ],
        compiler_params=pltpu.CompilerParams(
            collective_id=1, has_side_effects=True, vmem_limit_bytes=VMEM_LIMIT
        ),
        name="sweeps",
    )(probes, slow, absorb, partition)


def per_device(probes, slowness, absorbing, partition):
    flat = probes.reshape(PROBES, 2, 2, 32, 128).transpose(0, 1, 3, 2, 4).reshape(2 * PROBES * 64, 128)
    slow = slowness.reshape(2, 32, 128).transpose(1, 0, 2).reshape(64, 128)
    out, bases = swept(flat, slow, absorbing, partition.reshape(128, 128))
    field = out.reshape(PROBES, 2, 32, 2, 128).transpose(0, 1, 3, 2, 4).reshape(PROBES, 2, 2, 4096)
    return field, bases[None]


def solution(mesh):
    return jax.shard_map(
        per_device,
        mesh=mesh,
        in_specs=(P(None, None, "layer", "strip"), P("layer", "strip"), P("layer"), P()),
        out_specs=(P(None, None, "layer", "strip"), P(("layer", "strip"), None, None, None)),
        check_vma=False,
    )
```

```python
import functools

import jax
import jax.numpy as jnp
from jax import lax
from jax.experimental import pallas as pl
from jax.experimental.pallas import tpu as pltpu
from jax.sharding import PartitionSpec as P

ITERS = 9
BS = 64
SHIFTS = ((0, 0), (1, 0), (3, 0), (0, 1), (2, 0), (1, 1), (3, 1), (2, 1))
TAKE = (2, 2, 2, 2, 0, 0, 0, 0, 0, 0)
LAST = 1
WINDOW = 16
BLOCK = 8
OMEGA = 0.8
BETA = 0.5
SIGMA = 1.5

MESH = pl.DeviceIdType.MESH
PLANE = 32
GROUP = 8
PROBES = 16
PAIR = 2
OWN = 2 * GROUP
HALO = 8
ROWS = OWN + 2 * HALO
MAIN = 4
WIDE = 6
POS = 64
F32 = jnp.float32
VMEM_LIMIT = 62 * 1024 * 1024


def lanes():
    return lax.broadcasted_iota(jnp.int32, (8, 128), 1)


def sublanes():
    return lax.broadcasted_iota(jnp.int32, (8, 128), 0)


def widen(tiles, left, right, left_at, right_at):
    lane = lanes()
    first, last = tiles[0], tiles[3]
    before = jnp.where(lane < 32, pltpu.roll(last, 33, 1), pltpu.roll(last, 32, 1))
    before = jnp.where(lane == 0, pltpu.roll(left, (128 - left_at) % 128, 1), before)
    after = jnp.where(lane < 96, pltpu.roll(first, 96, 1), pltpu.roll(first, 95, 1))
    after = jnp.where(lane == 127, pltpu.roll(right, (255 - right_at) % 128, 1), after)
    return [before] + list(tiles) + [after]


def swap_blocks(v):
    lane = lanes()
    low, even = lane < 64, (lane & 32) == 0
    a = [None] * 4
    for h in range(2):
        a[h] = jnp.where(low, v[h], pltpu.roll(v[h + 2], 64, 1))
        a[h + 2] = jnp.where(low, pltpu.roll(v[h], 64, 1), v[h + 2])
    out = [None] * 4
    for h in (0, 2):
        out[h] = jnp.where(even, a[h], pltpu.roll(a[h + 1], 32, 1))
        out[h + 1] = jnp.where(even, pltpu.roll(a[h], 96, 1), a[h + 1])
    return out


def to_lanes(chunks):
    turned = jnp.concatenate(chunks, axis=0).T
    by_tile = [swap_blocks([turned[32 * h + 8 * j : 32 * h + 8 * j + 8] for h in range(4)]) for j in range(MAIN)]
    return [[by_tile[j][n] for j in range(MAIN)] for n in range(4)]


def to_chunks(rows):
    by_tile = [swap_blocks([rows[n][j] for n in range(4)]) for j in range(MAIN)]
    return jnp.concatenate([by_tile[j][h] for h in range(4) for j in range(MAIN)], axis=0).T


def kernel(
    probes, slow, absorb, partition,
    field, bases,
    inbuf, slowbuf, flags, esend, erecv, sendf, ssend, epack, fbuf, sbuf, ebuf, coef, gbuf, ubuf, vbuf, obuf, rbuf,
    points, tsend, tbuf, picked, gat, mats,
    in_sem, es, er, own_sem, fs, fr, zs, zr, rs, rr,
    ts, tr, town, gs, gr, gown,
):
    layer = lax.axis_index("layer")
    strip = lax.axis_index("strip")
    z = layer // GROUP
    me = lax.rem(layer, GROUP)

    mine_x, mine_y = lax.rem(me, 4), me // 4

    def peer_of(j):
        dx, dy = SHIFTS[j]
        return lax.rem(mine_y + dy, 2) * 4 + lax.rem(mine_x + dx, 4)

    def from_of(j):
        dx, dy = SHIFTS[j]
        return lax.rem(mine_y + dy, 2) * 4 + lax.rem(mine_x + 4 - dx, 4)

    def member(m):
        return (z * GROUP + m, strip)

    place = me * 4 + strip

    def in_plane(d):
        return (z * GROUP + d // 4, lax.rem(d, 4))

    up_id = (layer - GROUP, strip)
    down_id = (layer + GROUP, strip)

    copies = [
        pltpu.make_async_copy(probes, inbuf, in_sem.at[0]),
        pltpu.make_async_copy(slow, slowbuf, in_sem.at[1]),
        pltpu.make_async_copy(absorb, flags, in_sem.at[2]),
        pltpu.make_async_copy(partition.at[pl.ds(16 * z, 16)], points, in_sem.at[3]),
    ]
    for c in copies:
        c.start()

    barrier = pltpu.get_barrier_semaphore()
    for j in range(1, PLANE):
        pl.semaphore_signal(barrier, inc=1, device_id=in_plane(lax.rem(place + j, PLANE)), device_id_type=MESH)

    def meets(other):
        return (z == 3) | (z == 4) | (other == 3) | (other == 4) | (other == z + 1) | (other == z - 1)

    greeted = PLANE - 1
    for dz in range(1, 8):
        other = lax.rem(z + dz, 8)
        greeted = greeted + jnp.where(meets(other), 1, 0)

        @pl.when(meets(other))
        def _():
            pl.semaphore_signal(barrier, inc=1, device_id=(other * GROUP + me, strip), device_id_type=MESH)

    @pl.when(strip == 0)
    def _():
        erecv[0] = jnp.zeros_like(erecv[0])

    @pl.when(strip == 3)
    def _():
        erecv[1] = jnp.zeros_like(erecv[1])

    @pl.when(z == 0)
    def _():
        for p in range(PAIR):
            fbuf[p, 0:HALO] = jnp.zeros((HALO, 2, MAIN, 8, 128), F32)
        sbuf[0:HALO] = jnp.zeros((HALO, MAIN, 8, 128), F32)
        ebuf[0:4] = jnp.zeros((4, 4, 8, 128), F32)

    @pl.when(z == 7)
    def _():
        for p in range(PAIR):
            fbuf[p, HALO + OWN : ROWS] = jnp.zeros((HALO, 2, MAIN, 8, 128), F32)
        sbuf[HALO + OWN : ROWS] = jnp.zeros((HALO, MAIN, 8, 128), F32)
        ebuf[12:16] = jnp.zeros((4, 4, 8, 128), F32)

    for c in copies:
        c.wait()

    for side, chunk in ((0, 0), (1, 31)):
        rows = []
        for r in range(2):
            at = 2 * chunk + r
            rows += [inbuf[pl.ds(512 * q + at, 8, stride=64), :] for q in range(4)]
            rows.append(jnp.broadcast_to(slowbuf[at : at + 1, :], (8, 128)))
        rows.append(jnp.zeros((48, 128), F32))
        turned = jnp.concatenate(rows, axis=0).T
        esend[side] = turned[0:8] if side == 0 else turned[120:128]

    def stage_f(p):
        for m in range(GROUP):
            base = (2 * m + p) * 128
            four = to_lanes([inbuf[pl.ds(base + 64 * c + r, 32, stride=2), :] for r in range(2) for c in range(2)])
            for r in range(2):
                for c in range(2):
                    for t in range(MAIN):
                        sendf[p, m, r, c, t] = four[2 * r + c][t]

    def stage_s():
        two = [slowbuf[pl.ds(r, 32, stride=2), :] for r in range(2)]
        four = to_lanes(two + two)
        for r in range(2):
            for t in range(MAIN):
                ssend[r, t] = four[r][t]

    stage_f(0)
    stage_s()
    stage_f(1)
    pl.semaphore_wait(barrier, greeted)

    def edge_copy(side, to):
        return pltpu.make_async_remote_copy(
            src_ref=esend.at[side], dst_ref=erecv.at[1 - side], send_sem=es.at[side], recv_sem=er.at[1 - side],
            device_id=(layer, to), device_id_type=MESH,
        )

    @pl.when(strip > 0)
    def _():
        edge_copy(0, strip - 1).start()

    @pl.when(strip < 3)
    def _():
        edge_copy(1, strip + 1).start()

    def rows_of(m):
        return pl.ds(HALO + 2 * m, 2)

    def f_copy(p, j, dst_member, to):
        return pltpu.make_async_remote_copy(
            src_ref=sendf.at[p, to], dst_ref=fbuf.at[p, rows_of(dst_member)], send_sem=fs.at[p, j], recv_sem=fr.at[p, j],
            device_id=member(to), device_id_type=MESH,
        )

    def s_copy(j, dst_member, to):
        return pltpu.make_async_remote_copy(
            src_ref=ssend, dst_ref=sbuf.at[rows_of(dst_member)], send_sem=fs.at[2, j], recv_sem=fr.at[2, j],
            device_id=member(to), device_id_type=MESH,
        )

    def e_copy(j, dst_member, to):
        return pltpu.make_async_remote_copy(
            src_ref=epack, dst_ref=ebuf.at[4 + dst_member], send_sem=fs.at[3, j], recv_sem=fr.at[3, j],
            device_id=member(to), device_id_type=MESH,
        )

    def own_f(p):
        return pltpu.make_async_copy(sendf.at[p, me], fbuf.at[p, rows_of(me)], own_sem.at[p])

    own_s = pltpu.make_async_copy(ssend, sbuf.at[rows_of(me)], own_sem.at[2])
    own_e = pltpu.make_async_copy(epack, ebuf.at[4 + me], own_sem.at[5])

    def stage_e():
        for side in range(2):
            epack[side] = erecv[side]
        for r in range(2):
            epack[2 + r] = jnp.full((8, 128), flags[r], jnp.int32).astype(F32)

    def launch(k, j):
        if j == 0:
            (own_e if k == 3 else own_s if k == 2 else own_f(k)).start()
        elif k == 3:
            e_copy(j, me, peer_of(j)).start()
        elif k == 2:
            s_copy(j, me, peer_of(j)).start()
        else:
            f_copy(k, j, me, peer_of(j)).start()

    early = [(0, j) for j in range(GROUP)] + [(2, j) for j in range(GROUP)] + [(3, j) for j in range(GROUP)]
    late = [(1, j) for j in range(GROUP)]
    queue = early + late

    ready = min(WINDOW + 1, 2 * GROUP)
    for k, j in queue[:ready]:
        launch(k, j)

    @pl.when(strip > 0)
    def _():
        edge_copy(0, strip - 1).wait_send()
        edge_copy(1, strip - 1).wait_recv()

    @pl.when(strip < 3)
    def _():
        edge_copy(1, strip + 1).wait_send()
        edge_copy(0, strip + 1).wait_recv()

    stage_e()
    for k, j in queue[ready : WINDOW + 1]:
        launch(k, j)

    def forward_ref(k, pair):
        return ebuf.at[pair] if k == 3 else (sbuf if k == 2 else fbuf.at[k]).at[pl.ds(2 * pair, 2)]

    def up_copy(k, j, m):
        return pltpu.make_async_remote_copy(
            src_ref=forward_ref(k, 4 + m), dst_ref=forward_ref(k, 12 + m),
            send_sem=zs.at[k, j], recv_sem=zr.at[k, j], device_id=up_id, device_id_type=MESH,
        )

    def down_copy(k, j, m):
        return pltpu.make_async_remote_copy(
            src_ref=forward_ref(k, 4 + m), dst_ref=forward_ref(k, m - 4),
            send_sem=zs.at[k, j], recv_sem=zr.at[k, j], device_id=down_id, device_id_type=MESH,
        )

    def arrive(k, j):
        m = from_of(j)
        if j == 0:
            (own_e if k == 3 else own_s if k == 2 else own_f(k)).wait()
        elif k == 2:
            s_copy(j, m, peer_of(j)).wait_recv()
        elif k == 3:
            e_copy(j, m, peer_of(j)).wait_recv()
        else:
            f_copy(k, j, m, peer_of(j)).wait_recv()

        @pl.when((m < 4) & (z > 0))
        def _():
            up_copy(k, j, m).start()

        @pl.when((m >= 4) & (z < 7))
        def _():
            down_copy(k, j, m).start()

    def halo_wait(k):
        for j in range(GROUP):
            m = from_of(j)

            @pl.when((m < 4) & (z < 7))
            def _():
                up_copy(k, j, m).wait_recv()

            @pl.when((m >= 4) & (z > 0))
            def _():
                down_copy(k, j, m).wait_recv()

    def advance(i):
        arrive(*queue[i])
        if i + WINDOW + 1 < len(queue):
            launch(*queue[i + WINDOW + 1])

    for i in range(len(early)):
        advance(i)
    halo_wait(2)
    halo_wait(3)

    def by_pairs(work):
        def two(i, carry):
            for n in range(2):
                work(2 * i + n)
            return carry

        lax.fori_loop(0, ROWS // 4, two, 0)

    def coef_pair(pair):
        lane = lanes()
        left, right = ebuf[pair, 0], ebuf[pair, 1]
        inside = ((pair >= 4) | (z > 0)) & ((pair < 12) | (z < 7))
        for n in range(2):
            r = 2 * pair + n
            flag = ebuf[pair, 2 + n]
            wide = widen([sbuf[r, t] for t in range(MAIN)], left, right, 40 * n + 32, 40 * n + 32)
            for t in range(WIDE):
                dre = 4.0 - wide[t]
                dim = BETA * wide[t] + SIGMA * flag
                scale = OMEGA / (dre * dre + dim * dim)
                keep = jnp.full((8, 128), inside)
                if t == 0:
                    keep = keep & ((lane > 0) | jnp.full((8, 128), strip > 0))
                if t == WIDE - 1:
                    keep = keep & ((lane < 127) | jnp.full((8, 128), strip < 3))
                coef[r, 0, 8 + 8 * t : 16 + 8 * t] = jnp.where(keep, dre * scale, 0.0)
                coef[r, 1, 8 + 8 * t : 16 + 8 * t] = jnp.where(keep, -dim * scale, 0.0)

    by_pairs(coef_pair)
    halo_wait(0)

    def source_row(p):
        def pair_of(pair):
            left = pltpu.roll(ebuf[pair, 0], lax.rem(128 - 4 * me, 128), 1)
            right = pltpu.roll(ebuf[pair, 1], lax.rem(128 - 4 * me, 128), 1)
            for n in range(2):
                r = 2 * pair + n
                wide = []
                for c in range(2):
                    at = 40 * n + 2 * p + c
                    wide.append(widen([fbuf[p, r, c, t] for t in range(MAIN)], left, right, at, at))
                for t in range(WIDE):
                    at = slice(8 + 8 * t, 16 + 8 * t)
                    er_, ei_ = coef[r, 0, at], coef[r, 1, at]
                    fr_, fi_ = wide[0][t], wide[1][t]
                    gbuf[p, r, 0, at] = er_ * fr_ - ei_ * fi_
                    gbuf[p, r, 1, at] = er_ * fi_ + ei_ * fr_

        by_pairs(pair_of)

    def sweep(p, step, middle=None):
        src = gbuf if step == 2 else (ubuf if step % 2 else vbuf)
        dst = vbuf if step % 2 else ubuf
        start, tiles = (8, 6) if step < 5 else (12, 5) if step < ITERS else (16, 4)
        if middle is None:
            low, count = step - 1, ROWS + 2 - 2 * step
            block = {30: 5, 28: 4, 26: 2, 24: 4, 22: 2, 20: 4, 18: 3, 16: 4}[count]
        else:
            low, count = middle - (ITERS - step), 2 * (ITERS - step) + 1
            block = {15: 5, 13: 1, 11: 1, 9: 3, 7: 1, 5: 5, 3: 3, 1: 1}[count]
        spans = [slice(start + 8 * t, start + 8 * t + 8) for t in range(tiles)]

        def load(r):
            return [src[p, r, c, at] for c in range(2) for at in spans]

        def body(i, carry):
            above, here = list(carry[: 2 * tiles]), list(carry[2 * tiles :])
            for n in range(block):
                r = low + block * i + n
                below = load(r + 1)
                near = [
                    src[p, r, c, at.start - 1 : at.stop - 1] + src[p, r, c, at.start + 1 : at.stop + 1]
                    for c in range(2)
                    for at in spans
                ]
                for t, at in enumerate(spans):
                    er_, ei_ = coef[r, 0, at], coef[r, 1, at]
                    nr = above[t] + below[t] + near[t]
                    ni = above[tiles + t] + below[tiles + t] + near[tiles + t]
                    new_r = (1.0 - OMEGA) * here[t] + gbuf[p, r, 0, at] + (er_ * nr - ei_ * ni)
                    new_i = (1.0 - OMEGA) * here[tiles + t] + gbuf[p, r, 1, at] + (er_ * ni + ei_ * nr)
                    if step < ITERS:
                        dst[p, r, 0, at], dst[p, r, 1, at] = new_r, new_i
                    elif middle is None:
                        obuf[p, r - HALO, 0, t], obuf[p, r - HALO, 1, t] = new_r, new_i
                    else:
                        tsend[0, t], tsend[1, t] = new_r, new_i
                above, here = here, below
            return tuple(above) + tuple(here)

        lax.fori_loop(0, count // block, body, tuple(load(low - 1)) + tuple(load(low)))

    def back_copy(p, j, of_member, to):
        return pltpu.make_async_remote_copy(
            src_ref=obuf.at[p, pl.ds(2 * to, 2)], dst_ref=rbuf.at[2 * of_member + p], send_sem=rs.at[p, j], recv_sem=rr.at[p, j],
            device_id=member(to), device_id_type=MESH,
        )

    def own_back(p):
        return pltpu.make_async_copy(obuf.at[p, pl.ds(2 * me, 2)], rbuf.at[2 * me + p], own_sem.at[3 + p])

    def send_back(p):
        for j in range(1, GROUP):
            back_copy(p, j, me, peer_of(j)).start()
        own_back(p).start()

    def receive_back(p):
        for first in (0, 4):
            for j in range(first, first + 4):
                if j == 0:
                    own_back(p).wait()
                else:
                    back_copy(p, j, from_of(j), peer_of(j)).wait_recv()
            for j in range(first, first + 4):
                q = 2 * from_of(j) + p
                rows = to_chunks([[rbuf[q, r, c, t] for t in range(MAIN)] for r in range(2) for c in range(2)])
                for r in range(2):
                    for c in range(2):
                        n = 2 * r + c
                        field[pl.ds(q * 128 + 64 * c + r, 32, stride=2), :] = rows[32 * n : 32 * n + 32]

    def trace_row(side, p):
        return tsend if p else obuf.at[p, OWN - 1 if side == 0 else 0]

    def trace_copy(side, p, other):
        return pltpu.make_async_remote_copy(
            src_ref=trace_row(side, p), dst_ref=tbuf.at[side, p],
            send_sem=ts.at[p, other], recv_sem=tr.at[side, p],
            device_id=(other * GROUP + me, strip), device_id_type=MESH,
        )

    def trace_own(side, p):
        return pltpu.make_async_copy(trace_row(side, p), tbuf.at[side, p], town.at[p])

    def trace_send(p):
        for side in range(2):
            owner = 3 + side

            @pl.when(z == owner)
            def _():
                for other in range(8):
                    if other == owner:
                        trace_own(side, p).start()
                    else:
                        trace_copy(side, p, other).start()

    def trace_wait(p):
        for side in range(2):
            owner = 3 + side

            @pl.when(z == owner)
            def _():
                trace_own(side, p).wait()

            @pl.when(z != owner)
            def _():
                trace_copy(side, p, 0).wait_recv()

    def pick(p, g):
        sub = sublanes()
        at = jnp.broadcast_to(points[pl.ds(g, 1), :], (8, 128)) - strip * 4096
        tile, lane = (at >> 3) & 3, (at & 96) | ((at >> 7) & 31)
        hit = ((at >> 12) == 0) & ((at & 7) == sub)
        rows = jnp.zeros((8, 128), F32) if p == 0 else picked[g]
        for side in range(2):
            for c in range(2):
                got = [jnp.take_along_axis(tbuf[side, p, c, t], lane, axis=1) for t in range(MAIN)]
                best = got[0]
                for t in range(1, MAIN):
                    best = jnp.where(tile == t, got[t], best)
                one = jnp.sum(jnp.where(hit, best, 0.0), axis=0, keepdims=True)
                rows = jnp.where(sub == side * 4 + p * 2 + c, jnp.broadcast_to(one, (8, 128)), rows)
        picked[g] = rows

    def pick_all(p):
        def four(i, carry):
            for n in range(4):
                pick(p, 4 * i + n)
            return carry

        lax.fori_loop(0, 4, four, 0)

    def picked_copy(j, source, to):
        return pltpu.make_async_remote_copy(
            src_ref=picked.at[to // 2], dst_ref=gat.at[source], send_sem=gs.at[j], recv_sem=gr.at[j],
            device_id=in_plane(to), device_id_type=MESH,
        )

    picked_own = pltpu.make_async_copy(picked.at[place // 2], gat.at[place], gown)

    def pick_send():
        pick_all(1)
        for j in range(1, PLANE):
            picked_copy(j, place, lax.rem(place + j, PLANE)).start()
        picked_own.start()

    def compress():
        for j in range(1, PLANE):
            picked_copy(j, lax.rem(place + PLANE - j, PLANE), lax.rem(place + j, PLANE)).wait_recv()
        picked_own.wait()
        lane32 = lax.broadcasted_iota(jnp.int32, (32, 128), 1)
        row32 = lax.broadcasted_iota(jnp.int32, (32, 128), 0)
        odd = jnp.full((8, 128), lax.rem(strip, 2) == 1)
        for m in range(GROUP):
            tile = (gat[4 * m] + gat[4 * m + 1]) + (gat[4 * m + 2] + gat[4 * m + 3])
            tile = jnp.where(odd, pltpu.roll(tile, 64, 1), tile)
            tile = jnp.where(lanes() < 64, tile, 0.0)
            for side in range(2):
                mats[side, 4 * m : 4 * m + 4, :] = tile[4 * side : 4 * side + 4, :]
        augmented = []
        for side in range(2):
            mat = mats[side]
            zero = jnp.zeros((32, 128), F32)
            spread = jnp.concatenate([zero, zero, mat, zero], axis=0)
            gram = lax.dot_general(
                mat, spread, (((1,), (1,)), ((), ())), precision=lax.Precision.HIGHEST, preferred_element_type=F32
            )
            augmented.append(jnp.where(lane32 < 64, mat, gram))
        for first in range(0, 32, BLOCK):
            spread = [
                [jnp.broadcast_to(a[:, 64 + k : 65 + k], (32, 128)) for k in range(first, first + BLOCK)] for a in augmented
            ]
            for j in range(BLOCK):
                k = first + j
                for side in range(2):
                    a, columns = augmented[side], spread[side]
                    inverse = lax.rsqrt(jnp.broadcast_to(columns[j][k : k + 1, :], (32, 128)))
                    row = jnp.broadcast_to(a[k : k + 1, :], (32, 128)) * inverse
                    column = columns[j] * inverse
                    augmented[side] = jnp.where(row32 > k, a - column * row, jnp.where(row32 == k, row, a))
                    for i in range(j + 1, BLOCK):
                        across = jnp.broadcast_to(columns[i][k : k + 1, :], (32, 128)) * inverse
                        columns[i] = columns[i] - column * across
        for side in range(2):
            bases[side] = augmented[side][:, :BS]

    later = iter(range(len(early), len(queue)))

    def take(n):
        for _ in range(n):
            advance(next(later))

    take(TAKE[0])
    source_row(0)
    take(TAKE[1])
    for step in range(2, ITERS + 1):
        sweep(0, step)
        take(TAKE[step])
    trace_send(0)
    send_back(0)
    halo_wait(1)
    source_row(1)

    @pl.when((z == 3) | (z == 4))
    def _():
        for step in range(2, ITERS + 1):
            sweep(1, step, jnp.where(z == 3, HALO + OWN - 1, HALO))
        trace_send(1)

    for step in range(2, ITERS + 1):
        sweep(1, step)
    send_back(1)
    trace_wait(0)
    pick_all(0)
    receive_back(0)
    trace_wait(1)
    pick_send()
    if LAST == 0:
        compress()
    receive_back(1)
    if LAST == 1:
        compress()

    for j in range(1, GROUP):
        for p in range(PAIR):
            f_copy(p, j, me, peer_of(j)).wait_send()
            back_copy(p, j, me, peer_of(j)).wait_send()
        s_copy(j, me, peer_of(j)).wait_send()
        e_copy(j, me, peer_of(j)).wait_send()
    for k in range(4):
        for j in range(GROUP):
            m = from_of(j)

            @pl.when((m < 4) & (z > 0))
            def _():
                up_copy(k, j, m).wait_send()

            @pl.when((m >= 4) & (z < 7))
            def _():
                down_copy(k, j, m).wait_send()

    for p in range(PAIR):
        for side in range(2):

            @pl.when(z == 3 + side)
            def _():
                for other in range(8):
                    if other != 3 + side:
                        trace_copy(side, p, other).wait_send()

    for j in range(1, PLANE):
        picked_copy(j, place, lax.rem(place + j, PLANE)).wait_send()


def swept(probes, slow, absorb, partition):
    far = pl.BlockSpec(memory_space=pltpu.HBM)
    near = pl.BlockSpec(memory_space=pltpu.VMEM)
    dma = pltpu.SemaphoreType.DMA
    return pl.pallas_call(
        kernel,
        out_shape=(
            jax.ShapeDtypeStruct((2 * PROBES * 64, 128), F32),
            jax.ShapeDtypeStruct((2, 2 * PROBES, BS), F32),
        ),
        in_specs=[far] * 4,
        out_specs=(near, near),
        scratch_shapes=[
            pltpu.VMEM((2 * PROBES * 64, 128), F32),
            pltpu.VMEM((64, 128), F32),
            pltpu.SMEM((2,), jnp.int32),
            pltpu.VMEM((2, 8, 128), F32),
            pltpu.VMEM((2, 8, 128), F32),
            pltpu.VMEM((PAIR, GROUP, 2, 2, MAIN, 8, 128), F32),
            pltpu.VMEM((2, MAIN, 8, 128), F32),
            pltpu.VMEM((4, 8, 128), F32),
            pltpu.VMEM((PAIR, ROWS, 2, MAIN, 8, 128), F32),
            pltpu.VMEM((ROWS, MAIN, 8, 128), F32),
            pltpu.VMEM((ROWS // 2, 4, 8, 128), F32),
            pltpu.VMEM((ROWS, 2, POS, 128), F32),
            pltpu.VMEM((PAIR, ROWS, 2, POS, 128), F32),
            pltpu.VMEM((PAIR, ROWS, 2, POS, 128), F32),
            pltpu.VMEM((PAIR, ROWS, 2, POS, 128), F32),
            pltpu.VMEM((PAIR, OWN, 2, MAIN, 8, 128), F32),
            pltpu.VMEM((PROBES, 2, 2, MAIN, 8, 128), F32),
            pltpu.VMEM((16, 128), jnp.int32),
            pltpu.VMEM((2, MAIN, 8, 128), F32),
            pltpu.VMEM((2, PAIR, 2, MAIN, 8, 128), F32),
            pltpu.VMEM((16, 8, 128), F32),
            pltpu.VMEM((PLANE, 8, 128), F32),
            pltpu.VMEM((2, 32, 128), F32),
            dma((4,)),
            dma((2,)),
            dma((2,)),
            dma((6,)),
            dma((4, GROUP)),
            dma((4, GROUP)),
            dma((4, GROUP)),
            dma((4, GROUP)),
            dma((PAIR, GROUP)),
            dma((PAIR, GROUP)),
            dma((PAIR, 8)),
            dma((2, PAIR)),
            dma((PAIR,)),
            dma((PLANE,)),
            dma((PLANE,)),
            dma(()),
        ],
        compiler_params=pltpu.CompilerParams(
            collective_id=1, has_side_effects=True, vmem_limit_bytes=VMEM_LIMIT
        ),
        name="sweeps",
    )(probes, slow, absorb, partition)


def per_device(probes, slowness, absorbing, partition):
    flat = probes.reshape(PROBES, 2, 2, 32, 128).transpose(0, 1, 3, 2, 4).reshape(2 * PROBES * 64, 128)
    slow = slowness.reshape(2, 32, 128).transpose(1, 0, 2).reshape(64, 128)
    out, bases = swept(flat, slow, absorbing, partition.reshape(128, 128))
    field = out.reshape(PROBES, 2, 32, 2, 128).transpose(0, 1, 3, 2, 4).reshape(PROBES, 2, 2, 4096)
    return field, bases[None]


def solution(mesh):
    return jax.shard_map(
        per_device,
        mesh=mesh,
        in_specs=(P(None, None, "layer", "strip"), P("layer", "strip"), P("layer"), P()),
        out_specs=(P(None, None, "layer", "strip"), P(("layer", "strip"), None, None, None)),
        check_vma=False,
    )
```

```python
import functools

import jax
import jax.numpy as jnp
from jax import lax
from jax.experimental import pallas as pl
from jax.experimental.pallas import tpu as pltpu
from jax.sharding import PartitionSpec as P

ITERS = 9
BS = 64
SHIFTS = ((0, 0), (1, 0), (3, 0), (0, 1), (2, 0), (1, 1), (3, 1), (2, 1))
TAKE = (4, 4, 0, 0, 0, 0, 0, 0, 0, 0)
WINDOW = 22
BLOCK = 8
OMEGA = 0.8
BETA = 0.5
SIGMA = 1.5

MESH = pl.DeviceIdType.MESH
PLANE = 32
GROUP = 8
PROBES = 16
PAIR = 2
OWN = 2 * GROUP
HALO = 8
ROWS = OWN + 2 * HALO
MAIN = 4
WIDE = 6
POS = 64
F32 = jnp.float32
VMEM_LIMIT = 62 * 1024 * 1024


def lanes():
    return lax.broadcasted_iota(jnp.int32, (8, 128), 1)


def sublanes():
    return lax.broadcasted_iota(jnp.int32, (8, 128), 0)


def widen(tiles, left, right, left_at, right_at):
    lane = lanes()
    first, last = tiles[0], tiles[3]
    before = jnp.where(lane < 32, pltpu.roll(last, 33, 1), pltpu.roll(last, 32, 1))
    before = jnp.where(lane == 0, pltpu.roll(left, (128 - left_at) % 128, 1), before)
    after = jnp.where(lane < 96, pltpu.roll(first, 96, 1), pltpu.roll(first, 95, 1))
    after = jnp.where(lane == 127, pltpu.roll(right, (255 - right_at) % 128, 1), after)
    return [before] + list(tiles) + [after]


def swap_blocks(v):
    lane = lanes()
    low, even = lane < 64, (lane & 32) == 0
    a = [None] * 4
    for h in range(2):
        a[h] = jnp.where(low, v[h], pltpu.roll(v[h + 2], 64, 1))
        a[h + 2] = jnp.where(low, pltpu.roll(v[h], 64, 1), v[h + 2])
    out = [None] * 4
    for h in (0, 2):
        out[h] = jnp.where(even, a[h], pltpu.roll(a[h + 1], 32, 1))
        out[h + 1] = jnp.where(even, pltpu.roll(a[h], 96, 1), a[h + 1])
    return out


def to_lanes(chunks):
    turned = jnp.concatenate(chunks, axis=0).T
    by_tile = [swap_blocks([turned[32 * h + 8 * j : 32 * h + 8 * j + 8] for h in range(4)]) for j in range(MAIN)]
    return [[by_tile[j][n] for j in range(MAIN)] for n in range(4)]


def to_chunks(rows):
    by_tile = [swap_blocks([rows[n][j] for n in range(4)]) for j in range(MAIN)]
    return jnp.concatenate([by_tile[j][h] for h in range(4) for j in range(MAIN)], axis=0).T


def kernel(
    probes, slow, absorb, partition,
    field, bases,
    inbuf, slowbuf, flags, esend, erecv, sendf, ssend, epack, fbuf, sbuf, ebuf, coef, gbuf, ubuf, vbuf, obuf, rbuf,
    points, tsend, tbuf, picked, gat, mats,
    in_sem, es, er, own_sem, fs, fr, zs, zr, rs, rr,
    ts, tr, town, gs, gr, gown,
):
    layer = lax.axis_index("layer")
    strip = lax.axis_index("strip")
    z = layer // GROUP
    me = lax.rem(layer, GROUP)

    mine_x, mine_y = lax.rem(me, 4), me // 4

    def peer_of(j):
        dx, dy = SHIFTS[j]
        return lax.rem(mine_y + dy, 2) * 4 + lax.rem(mine_x + dx, 4)

    def from_of(j):
        dx, dy = SHIFTS[j]
        return lax.rem(mine_y + dy, 2) * 4 + lax.rem(mine_x + 4 - dx, 4)

    def member(m):
        return (z * GROUP + m, strip)

    place = me * 4 + strip

    def in_plane(d):
        return (z * GROUP + d // 4, lax.rem(d, 4))

    up_id = (layer - GROUP, strip)
    down_id = (layer + GROUP, strip)

    copies = [
        pltpu.make_async_copy(probes, inbuf, in_sem.at[0]),
        pltpu.make_async_copy(slow, slowbuf, in_sem.at[1]),
        pltpu.make_async_copy(absorb, flags, in_sem.at[2]),
        pltpu.make_async_copy(partition.at[pl.ds(16 * z, 16)], points, in_sem.at[3]),
    ]
    for c in copies:
        c.start()

    barrier = pltpu.get_barrier_semaphore()
    for j in range(1, PLANE):
        pl.semaphore_signal(barrier, inc=1, device_id=in_plane(lax.rem(place + j, PLANE)), device_id_type=MESH)

    def meets(other):
        return (z == 3) | (z == 4) | (other == 3) | (other == 4) | (other == z + 1) | (other == z - 1)

    greeted = PLANE - 1
    for dz in range(1, 8):
        other = lax.rem(z + dz, 8)
        greeted = greeted + jnp.where(meets(other), 1, 0)

        @pl.when(meets(other))
        def _():
            pl.semaphore_signal(barrier, inc=1, device_id=(other * GROUP + me, strip), device_id_type=MESH)

    @pl.when(strip == 0)
    def _():
        erecv[0] = jnp.zeros_like(erecv[0])

    @pl.when(strip == 3)
    def _():
        erecv[1] = jnp.zeros_like(erecv[1])

    @pl.when(z == 0)
    def _():
        for p in range(PAIR):
            fbuf[p, 0:HALO] = jnp.zeros((HALO, 2, MAIN, 8, 128), F32)
        sbuf[0:HALO] = jnp.zeros((HALO, MAIN, 8, 128), F32)
        ebuf[0:4] = jnp.zeros((4, 4, 8, 128), F32)

    @pl.when(z == 7)
    def _():
        for p in range(PAIR):
            fbuf[p, HALO + OWN : ROWS] = jnp.zeros((HALO, 2, MAIN, 8, 128), F32)
        sbuf[HALO + OWN : ROWS] = jnp.zeros((HALO, MAIN, 8, 128), F32)
        ebuf[12:16] = jnp.zeros((4, 4, 8, 128), F32)

    for c in copies:
        c.wait()

    for side, chunk in ((0, 0), (1, 31)):
        rows = []
        for r in range(2):
            at = 2 * chunk + r
            rows += [inbuf[pl.ds(512 * q + at, 8, stride=64), :] for q in range(4)]
            rows.append(jnp.broadcast_to(slowbuf[at : at + 1, :], (8, 128)))
        rows.append(jnp.zeros((48, 128), F32))
        turned = jnp.concatenate(rows, axis=0).T
        esend[side] = turned[0:8] if side == 0 else turned[120:128]

    def stage_f(p):
        for m in range(GROUP):
            base = (2 * m + p) * 128
            four = to_lanes([inbuf[pl.ds(base + 64 * c + r, 32, stride=2), :] for r in range(2) for c in range(2)])
            for r in range(2):
                for c in range(2):
                    for t in range(MAIN):
                        sendf[p, m, r, c, t] = four[2 * r + c][t]

    def stage_s():
        two = [slowbuf[pl.ds(r, 32, stride=2), :] for r in range(2)]
        four = to_lanes(two + two)
        for r in range(2):
            for t in range(MAIN):
                ssend[r, t] = four[r][t]

    stage_f(0)
    stage_s()
    stage_f(1)
    pl.semaphore_wait(barrier, greeted)

    def edge_copy(side, to):
        return pltpu.make_async_remote_copy(
            src_ref=esend.at[side], dst_ref=erecv.at[1 - side], send_sem=es.at[side], recv_sem=er.at[1 - side],
            device_id=(layer, to), device_id_type=MESH,
        )

    @pl.when(strip > 0)
    def _():
        edge_copy(0, strip - 1).start()

    @pl.when(strip < 3)
    def _():
        edge_copy(1, strip + 1).start()

    def rows_of(m):
        return pl.ds(HALO + 2 * m, 2)

    def f_copy(p, j, dst_member, to):
        return pltpu.make_async_remote_copy(
            src_ref=sendf.at[p, to], dst_ref=fbuf.at[p, rows_of(dst_member)], send_sem=fs.at[p, j], recv_sem=fr.at[p, j],
            device_id=member(to), device_id_type=MESH,
        )

    def s_copy(j, dst_member, to):
        return pltpu.make_async_remote_copy(
            src_ref=ssend, dst_ref=sbuf.at[rows_of(dst_member)], send_sem=fs.at[2, j], recv_sem=fr.at[2, j],
            device_id=member(to), device_id_type=MESH,
        )

    def e_copy(j, dst_member, to):
        return pltpu.make_async_remote_copy(
            src_ref=epack, dst_ref=ebuf.at[4 + dst_member], send_sem=fs.at[3, j], recv_sem=fr.at[3, j],
            device_id=member(to), device_id_type=MESH,
        )

    def own_f(p):
        return pltpu.make_async_copy(sendf.at[p, me], fbuf.at[p, rows_of(me)], own_sem.at[p])

    own_s = pltpu.make_async_copy(ssend, sbuf.at[rows_of(me)], own_sem.at[2])
    own_e = pltpu.make_async_copy(epack, ebuf.at[4 + me], own_sem.at[5])

    def stage_e():
        for side in range(2):
            epack[side] = erecv[side]
        for r in range(2):
            epack[2 + r] = jnp.full((8, 128), flags[r], jnp.int32).astype(F32)

    def launch(k, j):
        if j == 0:
            (own_e if k == 3 else own_s if k == 2 else own_f(k)).start()
        elif k == 3:
            e_copy(j, me, peer_of(j)).start()
        elif k == 2:
            s_copy(j, me, peer_of(j)).start()
        else:
            f_copy(k, j, me, peer_of(j)).start()

    early = [(0, j) for j in range(GROUP)] + [(2, j) for j in range(GROUP)] + [(3, j) for j in range(GROUP)]
    late = [(1, j) for j in range(GROUP)]
    queue = early + late

    ready = min(WINDOW + 1, 2 * GROUP)
    for k, j in queue[:ready]:
        launch(k, j)

    @pl.when(strip > 0)
    def _():
        edge_copy(0, strip - 1).wait_send()
        edge_copy(1, strip - 1).wait_recv()

    @pl.when(strip < 3)
    def _():
        edge_copy(1, strip + 1).wait_send()
        edge_copy(0, strip + 1).wait_recv()

    stage_e()
    for k, j in queue[ready : WINDOW + 1]:
        launch(k, j)

    def forward_ref(k, pair):
        return ebuf.at[pair] if k == 3 else (sbuf if k == 2 else fbuf.at[k]).at[pl.ds(2 * pair, 2)]

    def up_copy(k, j, m):
        return pltpu.make_async_remote_copy(
            src_ref=forward_ref(k, 4 + m), dst_ref=forward_ref(k, 12 + m),
            send_sem=zs.at[k, j], recv_sem=zr.at[k, j], device_id=up_id, device_id_type=MESH,
        )

    def down_copy(k, j, m):
        return pltpu.make_async_remote_copy(
            src_ref=forward_ref(k, 4 + m), dst_ref=forward_ref(k, m - 4),
            send_sem=zs.at[k, j], recv_sem=zr.at[k, j], device_id=down_id, device_id_type=MESH,
        )

    def arrive(k, j):
        m = from_of(j)
        if j == 0:
            (own_e if k == 3 else own_s if k == 2 else own_f(k)).wait()
        elif k == 2:
            s_copy(j, m, peer_of(j)).wait_recv()
        elif k == 3:
            e_copy(j, m, peer_of(j)).wait_recv()
        else:
            f_copy(k, j, m, peer_of(j)).wait_recv()

        @pl.when((m < 4) & (z > 0))
        def _():
            up_copy(k, j, m).start()

        @pl.when((m >= 4) & (z < 7))
        def _():
            down_copy(k, j, m).start()

    def halo_wait(k):
        for j in range(GROUP):
            m = from_of(j)

            @pl.when((m < 4) & (z < 7))
            def _():
                up_copy(k, j, m).wait_recv()

            @pl.when((m >= 4) & (z > 0))
            def _():
                down_copy(k, j, m).wait_recv()

    def advance(i):
        arrive(*queue[i])
        if i + WINDOW + 1 < len(queue):
            launch(*queue[i + WINDOW + 1])

    for i in range(len(early)):
        advance(i)
    halo_wait(2)
    halo_wait(3)

    def by_pairs(work):
        def two(i, carry):
            for n in range(2):
                work(2 * i + n)
            return carry

        lax.fori_loop(0, ROWS // 4, two, 0)

    def coef_pair(pair):
        lane = lanes()
        left, right = ebuf[pair, 0], ebuf[pair, 1]
        inside = ((pair >= 4) | (z > 0)) & ((pair < 12) | (z < 7))
        for n in range(2):
            r = 2 * pair + n
            flag = ebuf[pair, 2 + n]
            wide = widen([sbuf[r, t] for t in range(MAIN)], left, right, 40 * n + 32, 40 * n + 32)
            for t in range(WIDE):
                dre = 4.0 - wide[t]
                dim = BETA * wide[t] + SIGMA * flag
                scale = OMEGA / (dre * dre + dim * dim)
                keep = jnp.full((8, 128), inside)
                if t == 0:
                    keep = keep & ((lane > 0) | jnp.full((8, 128), strip > 0))
                if t == WIDE - 1:
                    keep = keep & ((lane < 127) | jnp.full((8, 128), strip < 3))
                coef[r, 0, 8 + 8 * t : 16 + 8 * t] = jnp.where(keep, dre * scale, 0.0)
                coef[r, 1, 8 + 8 * t : 16 + 8 * t] = jnp.where(keep, -dim * scale, 0.0)

    by_pairs(coef_pair)
    halo_wait(0)

    def source_row(p):
        def pair_of(pair):
            left = pltpu.roll(ebuf[pair, 0], lax.rem(128 - 4 * me, 128), 1)
            right = pltpu.roll(ebuf[pair, 1], lax.rem(128 - 4 * me, 128), 1)
            for n in range(2):
                r = 2 * pair + n
                wide = []
                for c in range(2):
                    at = 40 * n + 2 * p + c
                    wide.append(widen([fbuf[p, r, c, t] for t in range(MAIN)], left, right, at, at))
                for t in range(WIDE):
                    at = slice(8 + 8 * t, 16 + 8 * t)
                    er_, ei_ = coef[r, 0, at], coef[r, 1, at]
                    fr_, fi_ = wide[0][t], wide[1][t]
                    gbuf[p, r, 0, at] = er_ * fr_ - ei_ * fi_
                    gbuf[p, r, 1, at] = er_ * fi_ + ei_ * fr_

        by_pairs(pair_of)

    def sweep(p, step, middle=None):
        src = gbuf if step == 2 else (ubuf if step % 2 else vbuf)
        dst = vbuf if step % 2 else ubuf
        start, tiles = (8, 6) if step < 5 else (12, 5) if step < ITERS else (16, 4)
        if middle is None:
            low, count = step - 1, ROWS + 2 - 2 * step
            block = {30: 5, 28: 4, 26: 2, 24: 4, 22: 2, 20: 4, 18: 3, 16: 4}[count]
        else:
            low, count = middle - (ITERS - step), 2 * (ITERS - step) + 1
            block = {15: 5, 13: 1, 11: 1, 9: 3, 7: 1, 5: 5, 3: 3, 1: 1}[count]
        spans = [slice(start + 8 * t, start + 8 * t + 8) for t in range(tiles)]

        def load(r):
            return [src[p, r, c, at] for c in range(2) for at in spans]

        def body(i, carry):
            above, here = list(carry[: 2 * tiles]), list(carry[2 * tiles :])
            for n in range(block):
                r = low + block * i + n
                below = load(r + 1)
                near = [
                    src[p, r, c, at.start - 1 : at.stop - 1] + src[p, r, c, at.start + 1 : at.stop + 1]
                    for c in range(2)
                    for at in spans
                ]
                for t, at in enumerate(spans):
                    er_, ei_ = coef[r, 0, at], coef[r, 1, at]
                    nr = above[t] + below[t] + near[t]
                    ni = above[tiles + t] + below[tiles + t] + near[tiles + t]
                    new_r = (1.0 - OMEGA) * here[t] + gbuf[p, r, 0, at] + (er_ * nr - ei_ * ni)
                    new_i = (1.0 - OMEGA) * here[tiles + t] + gbuf[p, r, 1, at] + (er_ * ni + ei_ * nr)
                    if step < ITERS:
                        dst[p, r, 0, at], dst[p, r, 1, at] = new_r, new_i
                    elif middle is None:
                        obuf[p, r - HALO, 0, t], obuf[p, r - HALO, 1, t] = new_r, new_i
                    else:
                        tsend[0, t], tsend[1, t] = new_r, new_i
                above, here = here, below
            return tuple(above) + tuple(here)

        lax.fori_loop(0, count // block, body, tuple(load(low - 1)) + tuple(load(low)))

    def back_copy(p, j, of_member, to):
        return pltpu.make_async_remote_copy(
            src_ref=obuf.at[p, pl.ds(2 * to, 2)], dst_ref=rbuf.at[2 * of_member + p], send_sem=rs.at[p, j], recv_sem=rr.at[p, j],
            device_id=member(to), device_id_type=MESH,
        )

    def own_back(p):
        return pltpu.make_async_copy(obuf.at[p, pl.ds(2 * me, 2)], rbuf.at[2 * me + p], own_sem.at[3 + p])

    def send_back(p):
        for j in range(1, GROUP):
            back_copy(p, j, me, peer_of(j)).start()
        own_back(p).start()

    def receive_back(p):
        for first in (0, 4):
            for j in range(first, first + 4):
                if j == 0:
                    own_back(p).wait()
                else:
                    back_copy(p, j, from_of(j), peer_of(j)).wait_recv()
            for j in range(first, first + 4):
                q = 2 * from_of(j) + p
                rows = to_chunks([[rbuf[q, r, c, t] for t in range(MAIN)] for r in range(2) for c in range(2)])
                for r in range(2):
                    for c in range(2):
                        n = 2 * r + c
                        field[pl.ds(q * 128 + 64 * c + r, 32, stride=2), :] = rows[32 * n : 32 * n + 32]

    def trace_row(side, p):
        return tsend if p else obuf.at[p, OWN - 1 if side == 0 else 0]

    def trace_copy(side, p, other):
        return pltpu.make_async_remote_copy(
            src_ref=trace_row(side, p), dst_ref=tbuf.at[side, p],
            send_sem=ts.at[p, other], recv_sem=tr.at[side, p],
            device_id=(other * GROUP + me, strip), device_id_type=MESH,
        )

    def trace_own(side, p):
        return pltpu.make_async_copy(trace_row(side, p), tbuf.at[side, p], town.at[p])

    def trace_send(p):
        for side in range(2):
            owner = 3 + side

            @pl.when(z == owner)
            def _():
                for other in range(8):
                    if other == owner:
                        trace_own(side, p).start()
                    else:
                        trace_copy(side, p, other).start()

    def trace_wait(p):
        for side in range(2):
            owner = 3 + side

            @pl.when(z == owner)
            def _():
                trace_own(side, p).wait()

            @pl.when(z != owner)
            def _():
                trace_copy(side, p, 0).wait_recv()

    def pick(p, g):
        sub = sublanes()
        at = jnp.broadcast_to(points[pl.ds(g, 1), :], (8, 128)) - strip * 4096
        tile, lane = (at >> 3) & 3, (at & 96) | ((at >> 7) & 31)
        hit = ((at >> 12) == 0) & ((at & 7) == sub)
        rows = jnp.zeros((8, 128), F32) if p == 0 else picked[g]
        for side in range(2):
            for c in range(2):
                got = [jnp.take_along_axis(tbuf[side, p, c, t], lane, axis=1) for t in range(MAIN)]
                best = got[0]
                for t in range(1, MAIN):
                    best = jnp.where(tile == t, got[t], best)
                one = jnp.sum(jnp.where(hit, best, 0.0), axis=0, keepdims=True)
                rows = jnp.where(sub == side * 4 + p * 2 + c, jnp.broadcast_to(one, (8, 128)), rows)
        picked[g] = rows

    def pick_all(p):
        def four(i, carry):
            for n in range(4):
                pick(p, 4 * i + n)
            return carry

        lax.fori_loop(0, 4, four, 0)

    def picked_copy(j, source, to):
        return pltpu.make_async_remote_copy(
            src_ref=picked.at[to // 2], dst_ref=gat.at[source], send_sem=gs.at[j], recv_sem=gr.at[j],
            device_id=in_plane(to), device_id_type=MESH,
        )

    picked_own = pltpu.make_async_copy(picked.at[place // 2], gat.at[place], gown)

    def pick_send():
        pick_all(1)
        for j in range(1, PLANE):
            picked_copy(j, place, lax.rem(place + j, PLANE)).start()
        picked_own.start()

    def compress():
        for j in range(1, PLANE):
            picked_copy(j, lax.rem(place + PLANE - j, PLANE), lax.rem(place + j, PLANE)).wait_recv()
        picked_own.wait()
        lane32 = lax.broadcasted_iota(jnp.int32, (32, 128), 1)
        row32 = lax.broadcasted_iota(jnp.int32, (32, 128), 0)
        odd = jnp.full((8, 128), lax.rem(strip, 2) == 1)
        for m in range(GROUP):
            tile = (gat[4 * m] + gat[4 * m + 1]) + (gat[4 * m + 2] + gat[4 * m + 3])
            tile = jnp.where(odd, pltpu.roll(tile, 64, 1), tile)
            tile = jnp.where(lanes() < 64, tile, 0.0)
            for side in range(2):
                mats[side, 4 * m : 4 * m + 4, :] = tile[4 * side : 4 * side + 4, :]
        augmented = []
        for side in range(2):
            mat = mats[side]
            zero = jnp.zeros((32, 128), F32)
            spread = jnp.concatenate([zero, zero, mat, zero], axis=0)
            gram = lax.dot_general(
                mat, spread, (((1,), (1,)), ((), ())), precision=lax.Precision.HIGHEST, preferred_element_type=F32
            )
            augmented.append(jnp.where(lane32 < 64, mat, gram))
        for first in range(0, 32, BLOCK):
            spread = [
                [jnp.broadcast_to(a[:, 64 + k : 65 + k], (32, 128)) for k in range(first, first + BLOCK)] for a in augmented
            ]
            for j in range(BLOCK):
                k = first + j
                for side in range(2):
                    a, columns = augmented[side], spread[side]
                    inverse = lax.rsqrt(jnp.broadcast_to(columns[j][k : k + 1, :], (32, 128)))
                    row = jnp.broadcast_to(a[k : k + 1, :], (32, 128)) * inverse
                    column = columns[j] * inverse
                    augmented[side] = jnp.where(row32 > k, a - column * row, jnp.where(row32 == k, row, a))
                    for i in range(j + 1, BLOCK):
                        across = jnp.broadcast_to(columns[i][k : k + 1, :], (32, 128)) * inverse
                        columns[i] = columns[i] - column * across
        for side in range(2):
            bases[side] = augmented[side][:, :BS]

    later = iter(range(len(early), len(queue)))

    def take(n):
        for _ in range(n):
            advance(next(later))

    take(TAKE[0])
    source_row(0)
    take(TAKE[1])
    for step in range(2, ITERS + 1):
        sweep(0, step)
        take(TAKE[step])
    trace_send(0)
    send_back(0)
    halo_wait(1)
    source_row(1)

    @pl.when((z == 3) | (z == 4))
    def _():
        for step in range(2, ITERS + 1):
            sweep(1, step, jnp.where(z == 3, HALO + OWN - 1, HALO))
        trace_send(1)

    for step in range(2, ITERS + 1):
        sweep(1, step)
    send_back(1)
    trace_wait(0)
    pick_all(0)
    trace_wait(1)
    pick_send()
    receive_back(0)
    receive_back(1)
    compress()

    for j in range(1, GROUP):
        for p in range(PAIR):
            f_copy(p, j, me, peer_of(j)).wait_send()
            back_copy(p, j, me, peer_of(j)).wait_send()
        s_copy(j, me, peer_of(j)).wait_send()
        e_copy(j, me, peer_of(j)).wait_send()
    for k in range(4):
        for j in range(GROUP):
            m = from_of(j)

            @pl.when((m < 4) & (z > 0))
            def _():
                up_copy(k, j, m).wait_send()

            @pl.when((m >= 4) & (z < 7))
            def _():
                down_copy(k, j, m).wait_send()

    for p in range(PAIR):
        for side in range(2):

            @pl.when(z == 3 + side)
            def _():
                for other in range(8):
                    if other != 3 + side:
                        trace_copy(side, p, other).wait_send()

    for j in range(1, PLANE):
        picked_copy(j, place, lax.rem(place + j, PLANE)).wait_send()


def swept(probes, slow, absorb, partition):
    far = pl.BlockSpec(memory_space=pltpu.HBM)
    near = pl.BlockSpec(memory_space=pltpu.VMEM)
    dma = pltpu.SemaphoreType.DMA
    return pl.pallas_call(
        kernel,
        out_shape=(
            jax.ShapeDtypeStruct((2 * PROBES * 64, 128), F32),
            jax.ShapeDtypeStruct((2, 2 * PROBES, BS), F32),
        ),
        in_specs=[far] * 4,
        out_specs=(near, near),
        scratch_shapes=[
            pltpu.VMEM((2 * PROBES * 64, 128), F32),
            pltpu.VMEM((64, 128), F32),
            pltpu.SMEM((2,), jnp.int32),
            pltpu.VMEM((2, 8, 128), F32),
            pltpu.VMEM((2, 8, 128), F32),
            pltpu.VMEM((PAIR, GROUP, 2, 2, MAIN, 8, 128), F32),
            pltpu.VMEM((2, MAIN, 8, 128), F32),
            pltpu.VMEM((4, 8, 128), F32),
            pltpu.VMEM((PAIR, ROWS, 2, MAIN, 8, 128), F32),
            pltpu.VMEM((ROWS, MAIN, 8, 128), F32),
            pltpu.VMEM((ROWS // 2, 4, 8, 128), F32),
            pltpu.VMEM((ROWS, 2, POS, 128), F32),
            pltpu.VMEM((PAIR, ROWS, 2, POS, 128), F32),
            pltpu.VMEM((PAIR, ROWS, 2, POS, 128), F32),
            pltpu.VMEM((PAIR, ROWS, 2, POS, 128), F32),
            pltpu.VMEM((PAIR, OWN, 2, MAIN, 8, 128), F32),
            pltpu.VMEM((PROBES, 2, 2, MAIN, 8, 128), F32),
            pltpu.VMEM((16, 128), jnp.int32),
            pltpu.VMEM((2, MAIN, 8, 128), F32),
            pltpu.VMEM((2, PAIR, 2, MAIN, 8, 128), F32),
            pltpu.VMEM((16, 8, 128), F32),
            pltpu.VMEM((PLANE, 8, 128), F32),
            pltpu.VMEM((2, 32, 128), F32),
            dma((4,)),
            dma((2,)),
            dma((2,)),
            dma((6,)),
            dma((4, GROUP)),
            dma((4, GROUP)),
            dma((4, GROUP)),
            dma((4, GROUP)),
            dma((PAIR, GROUP)),
            dma((PAIR, GROUP)),
            dma((PAIR, 8)),
            dma((2, PAIR)),
            dma((PAIR,)),
            dma((PLANE,)),
            dma((PLANE,)),
            dma(()),
        ],
        compiler_params=pltpu.CompilerParams(
            collective_id=1, has_side_effects=True, vmem_limit_bytes=VMEM_LIMIT
        ),
        name="sweeps",
    )(probes, slow, absorb, partition)


def per_device(probes, slowness, absorbing, partition):
    flat = probes.reshape(PROBES, 2, 2, 32, 128).transpose(0, 1, 3, 2, 4).reshape(2 * PROBES * 64, 128)
    slow = slowness.reshape(2, 32, 128).transpose(1, 0, 2).reshape(64, 128)
    out, bases = swept(flat, slow, absorbing, partition.reshape(128, 128))
    field = out.reshape(PROBES, 2, 32, 2, 128).transpose(0, 1, 3, 2, 4).reshape(PROBES, 2, 2, 4096)
    return field, bases[None]


def solution(mesh):
    return jax.shard_map(
        per_device,
        mesh=mesh,
        in_specs=(P(None, None, "layer", "strip"), P("layer", "strip"), P("layer"), P()),
        out_specs=(P(None, None, "layer", "strip"), P(("layer", "strip"), None, None, None)),
        check_vma=False,
    )
```

```python
import functools

import jax
import jax.numpy as jnp
from jax import lax
from jax.experimental import pallas as pl
from jax.experimental.pallas import tpu as pltpu
from jax.sharding import PartitionSpec as P

ITERS = 9
BS = 64
SHIFTS = ((0, 0), (1, 0), (3, 0), (0, 1), (2, 0), (1, 1), (3, 1), (2, 1))
TAKE = (4, 4, 0, 0, 0, 0, 0, 0, 0, 0)
WINDOW = 22
BLOCK = 8
OMEGA = 0.8
BETA = 0.5
SIGMA = 1.5

MESH = pl.DeviceIdType.MESH
PLANE = 32
GROUP = 8
PROBES = 16
PAIR = 2
OWN = 2 * GROUP
HALO = 8
ROWS = OWN + 2 * HALO
MAIN = 4
WIDE = 6
POS = 64
F32 = jnp.float32
VMEM_LIMIT = 62 * 1024 * 1024


def lanes():
    return lax.broadcasted_iota(jnp.int32, (8, 128), 1)


def sublanes():
    return lax.broadcasted_iota(jnp.int32, (8, 128), 0)


def widen(tiles, left, right, left_at, right_at):
    lane = lanes()
    first, last = tiles[0], tiles[3]
    before = jnp.where(lane < 32, pltpu.roll(last, 33, 1), pltpu.roll(last, 32, 1))
    before = jnp.where(lane == 0, pltpu.roll(left, (128 - left_at) % 128, 1), before)
    after = jnp.where(lane < 96, pltpu.roll(first, 96, 1), pltpu.roll(first, 95, 1))
    after = jnp.where(lane == 127, pltpu.roll(right, (255 - right_at) % 128, 1), after)
    return [before] + list(tiles) + [after]


def swap_blocks(v):
    lane = lanes()
    low, even = lane < 64, (lane & 32) == 0
    a = [None] * 4
    for h in range(2):
        a[h] = jnp.where(low, v[h], pltpu.roll(v[h + 2], 64, 1))
        a[h + 2] = jnp.where(low, pltpu.roll(v[h], 64, 1), v[h + 2])
    out = [None] * 4
    for h in (0, 2):
        out[h] = jnp.where(even, a[h], pltpu.roll(a[h + 1], 32, 1))
        out[h + 1] = jnp.where(even, pltpu.roll(a[h], 96, 1), a[h + 1])
    return out


def to_lanes(chunks):
    turned = jnp.concatenate(chunks, axis=0).T
    by_tile = [swap_blocks([turned[32 * h + 8 * j : 32 * h + 8 * j + 8] for h in range(4)]) for j in range(MAIN)]
    return [[by_tile[j][n] for j in range(MAIN)] for n in range(4)]


def to_chunks(rows):
    by_tile = [swap_blocks([rows[n][j] for n in range(4)]) for j in range(MAIN)]
    return jnp.concatenate([by_tile[j][h] for h in range(4) for j in range(MAIN)], axis=0).T


def kernel(
    probes, slow, absorb, partition,
    field, bases,
    inbuf, slowbuf, flags, esend, erecv, sendf, ssend, epack, fbuf, sbuf, ebuf, coef, gbuf, ubuf, vbuf, obuf, rbuf,
    points, tsend, tbuf, picked, gat, mats,
    in_sem, es, er, own_sem, fs, fr, zs, zr, rs, rr,
    ts, tr, town, gs, gr, gown,
):
    layer = lax.axis_index("layer")
    strip = lax.axis_index("strip")
    z = layer // GROUP
    me = lax.rem(layer, GROUP)

    mine_x, mine_y = lax.rem(me, 4), me // 4

    def peer_of(j):
        dx, dy = SHIFTS[j]
        return lax.rem(mine_y + dy, 2) * 4 + lax.rem(mine_x + dx, 4)

    def from_of(j):
        dx, dy = SHIFTS[j]
        return lax.rem(mine_y + dy, 2) * 4 + lax.rem(mine_x + 4 - dx, 4)

    def member(m):
        return (z * GROUP + m, strip)

    place = me * 4 + strip

    def in_plane(d):
        return (z * GROUP + d // 4, lax.rem(d, 4))

    up_id = (layer - GROUP, strip)
    down_id = (layer + GROUP, strip)

    copies = [
        pltpu.make_async_copy(probes, inbuf, in_sem.at[0]),
        pltpu.make_async_copy(slow, slowbuf, in_sem.at[1]),
        pltpu.make_async_copy(absorb, flags, in_sem.at[2]),
        pltpu.make_async_copy(partition.at[pl.ds(16 * z, 16)], points, in_sem.at[3]),
    ]
    for c in copies:
        c.start()

    barrier = pltpu.get_barrier_semaphore()
    for j in range(1, PLANE):
        pl.semaphore_signal(barrier, inc=1, device_id=in_plane(lax.rem(place + j, PLANE)), device_id_type=MESH)

    def meets(other):
        return (z == 3) | (z == 4) | (other == 3) | (other == 4) | (other == z + 1) | (other == z - 1)

    greeted = PLANE - 1
    for dz in range(1, 8):
        other = lax.rem(z + dz, 8)
        greeted = greeted + jnp.where(meets(other), 1, 0)

        @pl.when(meets(other))
        def _():
            pl.semaphore_signal(barrier, inc=1, device_id=(other * GROUP + me, strip), device_id_type=MESH)

    @pl.when(strip == 0)
    def _():
        erecv[0] = jnp.zeros_like(erecv[0])

    @pl.when(strip == 3)
    def _():
        erecv[1] = jnp.zeros_like(erecv[1])

    @pl.when(z == 0)
    def _():
        for p in range(PAIR):
            fbuf[p, 0:HALO] = jnp.zeros((HALO, 2, MAIN, 8, 128), F32)
        sbuf[0:HALO] = jnp.zeros((HALO, MAIN, 8, 128), F32)
        ebuf[0:4] = jnp.zeros((4, 4, 8, 128), F32)

    @pl.when(z == 7)
    def _():
        for p in range(PAIR):
            fbuf[p, HALO + OWN : ROWS] = jnp.zeros((HALO, 2, MAIN, 8, 128), F32)
        sbuf[HALO + OWN : ROWS] = jnp.zeros((HALO, MAIN, 8, 128), F32)
        ebuf[12:16] = jnp.zeros((4, 4, 8, 128), F32)

    for c in copies:
        c.wait()

    for side, chunk in ((0, 0), (1, 31)):
        rows = []
        for r in range(2):
            at = 2 * chunk + r
            rows += [inbuf[pl.ds(512 * q + at, 8, stride=64), :] for q in range(4)]
            rows.append(jnp.broadcast_to(slowbuf[at : at + 1, :], (8, 128)))
        rows.append(jnp.zeros((48, 128), F32))
        turned = jnp.concatenate(rows, axis=0).T
        esend[side] = turned[0:8] if side == 0 else turned[120:128]

    def stage_f(p):
        for m in range(GROUP):
            base = (2 * m + p) * 128
            four = to_lanes([inbuf[pl.ds(base + 64 * c + r, 32, stride=2), :] for r in range(2) for c in range(2)])
            for r in range(2):
                for c in range(2):
                    for t in range(MAIN):
                        sendf[p, m, r, c, t] = four[2 * r + c][t]

    def stage_s():
        two = [slowbuf[pl.ds(r, 32, stride=2), :] for r in range(2)]
        four = to_lanes(two + two)
        for r in range(2):
            for t in range(MAIN):
                ssend[r, t] = four[r][t]

    stage_f(0)
    stage_s()
    stage_f(1)
    pl.semaphore_wait(barrier, greeted)

    def edge_copy(side, to):
        return pltpu.make_async_remote_copy(
            src_ref=esend.at[side], dst_ref=erecv.at[1 - side], send_sem=es.at[side], recv_sem=er.at[1 - side],
            device_id=(layer, to), device_id_type=MESH,
        )

    @pl.when(strip > 0)
    def _():
        edge_copy(0, strip - 1).start()

    @pl.when(strip < 3)
    def _():
        edge_copy(1, strip + 1).start()

    def rows_of(m):
        return pl.ds(HALO + 2 * m, 2)

    def f_copy(p, j, dst_member, to):
        return pltpu.make_async_remote_copy(
            src_ref=sendf.at[p, to], dst_ref=fbuf.at[p, rows_of(dst_member)], send_sem=fs.at[p, j], recv_sem=fr.at[p, j],
            device_id=member(to), device_id_type=MESH,
        )

    def s_copy(j, dst_member, to):
        return pltpu.make_async_remote_copy(
            src_ref=ssend, dst_ref=sbuf.at[rows_of(dst_member)], send_sem=fs.at[2, j], recv_sem=fr.at[2, j],
            device_id=member(to), device_id_type=MESH,
        )

    def e_copy(j, dst_member, to):
        return pltpu.make_async_remote_copy(
            src_ref=epack, dst_ref=ebuf.at[4 + dst_member], send_sem=fs.at[3, j], recv_sem=fr.at[3, j],
            device_id=member(to), device_id_type=MESH,
        )

    def own_f(p):
        return pltpu.make_async_copy(sendf.at[p, me], fbuf.at[p, rows_of(me)], own_sem.at[p])

    own_s = pltpu.make_async_copy(ssend, sbuf.at[rows_of(me)], own_sem.at[2])
    own_e = pltpu.make_async_copy(epack, ebuf.at[4 + me], own_sem.at[5])

    def stage_e():
        for side in range(2):
            epack[side] = erecv[side]
        for r in range(2):
            epack[2 + r] = jnp.full((8, 128), flags[r], jnp.int32).astype(F32)

    def launch(k, j):
        if j == 0:
            (own_e if k == 3 else own_s if k == 2 else own_f(k)).start()
        elif k == 3:
            e_copy(j, me, peer_of(j)).start()
        elif k == 2:
            s_copy(j, me, peer_of(j)).start()
        else:
            f_copy(k, j, me, peer_of(j)).start()

    early = [(0, j) for j in range(GROUP)] + [(2, j) for j in range(GROUP)] + [(3, j) for j in range(GROUP)]
    late = [(1, j) for j in range(GROUP)]
    queue = early + late

    ready = min(WINDOW + 1, 2 * GROUP)
    for k, j in queue[:ready]:
        launch(k, j)

    @pl.when(strip > 0)
    def _():
        edge_copy(0, strip - 1).wait_send()
        edge_copy(1, strip - 1).wait_recv()

    @pl.when(strip < 3)
    def _():
        edge_copy(1, strip + 1).wait_send()
        edge_copy(0, strip + 1).wait_recv()

    stage_e()
    for k, j in queue[ready : WINDOW + 1]:
        launch(k, j)

    def forward_ref(k, pair):
        return ebuf.at[pair] if k == 3 else (sbuf if k == 2 else fbuf.at[k]).at[pl.ds(2 * pair, 2)]

    def up_copy(k, j, m):
        return pltpu.make_async_remote_copy(
            src_ref=forward_ref(k, 4 + m), dst_ref=forward_ref(k, 12 + m),
            send_sem=zs.at[k, j], recv_sem=zr.at[k, j], device_id=up_id, device_id_type=MESH,
        )

    def down_copy(k, j, m):
        return pltpu.make_async_remote_copy(
            src_ref=forward_ref(k, 4 + m), dst_ref=forward_ref(k, m - 4),
            send_sem=zs.at[k, j], recv_sem=zr.at[k, j], device_id=down_id, device_id_type=MESH,
        )

    def arrive(k, j):
        m = from_of(j)
        if j == 0:
            (own_e if k == 3 else own_s if k == 2 else own_f(k)).wait()
        elif k == 2:
            s_copy(j, m, peer_of(j)).wait_recv()
        elif k == 3:
            e_copy(j, m, peer_of(j)).wait_recv()
        else:
            f_copy(k, j, m, peer_of(j)).wait_recv()

        @pl.when((m < 4) & (z > 0))
        def _():
            up_copy(k, j, m).start()

        @pl.when((m >= 4) & (z < 7))
        def _():
            down_copy(k, j, m).start()

    def halo_wait(k):
        for j in range(GROUP):
            m = from_of(j)

            @pl.when((m < 4) & (z < 7))
            def _():
                up_copy(k, j, m).wait_recv()

            @pl.when((m >= 4) & (z > 0))
            def _():
                down_copy(k, j, m).wait_recv()

    def advance(i):
        arrive(*queue[i])
        if i + WINDOW + 1 < len(queue):
            launch(*queue[i + WINDOW + 1])

    for i in range(len(early)):
        advance(i)
    halo_wait(2)
    halo_wait(3)

    def by_pairs(work, first=0, count=ROWS // 4):
        def two(i, carry):
            for n in range(2):
                work(2 * (first + i) + n)
            return carry

        lax.fori_loop(0, count, two, 0)

    def coef_pair(pair):
        lane = lanes()
        left, right = ebuf[pair, 0], ebuf[pair, 1]
        inside = ((pair >= 4) | (z > 0)) & ((pair < 12) | (z < 7))
        for n in range(2):
            r = 2 * pair + n
            flag = ebuf[pair, 2 + n]
            wide = widen([sbuf[r, t] for t in range(MAIN)], left, right, 40 * n + 32, 40 * n + 32)
            for t in range(WIDE):
                dre = 4.0 - wide[t]
                dim = BETA * wide[t] + SIGMA * flag
                scale = OMEGA / (dre * dre + dim * dim)
                keep = jnp.full((8, 128), inside)
                if t == 0:
                    keep = keep & ((lane > 0) | jnp.full((8, 128), strip > 0))
                if t == WIDE - 1:
                    keep = keep & ((lane < 127) | jnp.full((8, 128), strip < 3))
                coef[r, 0, 8 + 8 * t : 16 + 8 * t] = jnp.where(keep, dre * scale, 0.0)
                coef[r, 1, 8 + 8 * t : 16 + 8 * t] = jnp.where(keep, -dim * scale, 0.0)

    by_pairs(coef_pair)
    halo_wait(0)

    def source_row(p, first=0, count=ROWS // 4):
        def pair_of(pair):
            left = pltpu.roll(ebuf[pair, 0], lax.rem(128 - 4 * me, 128), 1)
            right = pltpu.roll(ebuf[pair, 1], lax.rem(128 - 4 * me, 128), 1)
            for n in range(2):
                r = 2 * pair + n
                wide = []
                for c in range(2):
                    at = 40 * n + 2 * p + c
                    wide.append(widen([fbuf[p, r, c, t] for t in range(MAIN)], left, right, at, at))
                for t in range(WIDE):
                    at = slice(8 + 8 * t, 16 + 8 * t)
                    er_, ei_ = coef[r, 0, at], coef[r, 1, at]
                    fr_, fi_ = wide[0][t], wide[1][t]
                    gbuf[p, r, 0, at] = er_ * fr_ - ei_ * fi_
                    gbuf[p, r, 1, at] = er_ * fi_ + ei_ * fr_

        by_pairs(pair_of, first, count)

    def sweep(p, step, middle=None):
        src = gbuf if step == 2 else (ubuf if step % 2 else vbuf)
        dst = vbuf if step % 2 else ubuf
        start, tiles = (8, 6) if step < 5 else (12, 5) if step < ITERS else (16, 4)
        if middle is None:
            low, count = step - 1, ROWS + 2 - 2 * step
            block = {30: 5, 28: 4, 26: 2, 24: 4, 22: 2, 20: 4, 18: 3, 16: 4}[count]
        else:
            low, count = middle - (ITERS - step), 2 * (ITERS - step) + 1
            block = {15: 5, 13: 1, 11: 1, 9: 3, 7: 1, 5: 5, 3: 3, 1: 1}[count]
        spans = [slice(start + 8 * t, start + 8 * t + 8) for t in range(tiles)]

        def load(r):
            return [src[p, r, c, at] for c in range(2) for at in spans]

        def body(i, carry):
            above, here = list(carry[: 2 * tiles]), list(carry[2 * tiles :])
            for n in range(block):
                r = low + block * i + n
                below = load(r + 1)
                near = [
                    src[p, r, c, at.start - 1 : at.stop - 1] + src[p, r, c, at.start + 1 : at.stop + 1]
                    for c in range(2)
                    for at in spans
                ]
                for t, at in enumerate(spans):
                    er_, ei_ = coef[r, 0, at], coef[r, 1, at]
                    nr = above[t] + below[t] + near[t]
                    ni = above[tiles + t] + below[tiles + t] + near[tiles + t]
                    new_r = (1.0 - OMEGA) * here[t] + gbuf[p, r, 0, at] + (er_ * nr - ei_ * ni)
                    new_i = (1.0 - OMEGA) * here[tiles + t] + gbuf[p, r, 1, at] + (er_ * ni + ei_ * nr)
                    if step < ITERS:
                        dst[p, r, 0, at], dst[p, r, 1, at] = new_r, new_i
                    elif middle is None:
                        obuf[p, r - HALO, 0, t], obuf[p, r - HALO, 1, t] = new_r, new_i
                    else:
                        tsend[0, t], tsend[1, t] = new_r, new_i
                above, here = here, below
            return tuple(above) + tuple(here)

        lax.fori_loop(0, count // block, body, tuple(load(low - 1)) + tuple(load(low)))

    def back_copy(p, j, of_member, to):
        return pltpu.make_async_remote_copy(
            src_ref=obuf.at[p, pl.ds(2 * to, 2)], dst_ref=rbuf.at[2 * of_member + p], send_sem=rs.at[p, j], recv_sem=rr.at[p, j],
            device_id=member(to), device_id_type=MESH,
        )

    def own_back(p):
        return pltpu.make_async_copy(obuf.at[p, pl.ds(2 * me, 2)], rbuf.at[2 * me + p], own_sem.at[3 + p])

    def send_back(p):
        for j in range(1, GROUP):
            back_copy(p, j, me, peer_of(j)).start()
        own_back(p).start()

    def receive_back(p):
        for first in (0, 4):
            for j in range(first, first + 4):
                if j == 0:
                    own_back(p).wait()
                else:
                    back_copy(p, j, from_of(j), peer_of(j)).wait_recv()
            for j in range(first, first + 4):
                q = 2 * from_of(j) + p
                rows = to_chunks([[rbuf[q, r, c, t] for t in range(MAIN)] for r in range(2) for c in range(2)])
                for r in range(2):
                    for c in range(2):
                        n = 2 * r + c
                        field[pl.ds(q * 128 + 64 * c + r, 32, stride=2), :] = rows[32 * n : 32 * n + 32]

    def trace_row(side, p):
        return tsend if p else obuf.at[p, OWN - 1 if side == 0 else 0]

    def trace_copy(side, p, other):
        return pltpu.make_async_remote_copy(
            src_ref=trace_row(side, p), dst_ref=tbuf.at[side, p],
            send_sem=ts.at[p, other], recv_sem=tr.at[side, p],
            device_id=(other * GROUP + me, strip), device_id_type=MESH,
        )

    def trace_own(side, p):
        return pltpu.make_async_copy(trace_row(side, p), tbuf.at[side, p], town.at[p])

    def trace_send(p):
        for side in range(2):
            owner = 3 + side

            @pl.when(z == owner)
            def _():
                for other in sorted(range(8), key=lambda n: -min((n - owner) % 8, (owner - n) % 8)):
                    if other == owner:
                        trace_own(side, p).start()
                    else:
                        trace_copy(side, p, other).start()

    def trace_wait(p):
        for side in range(2):
            owner = 3 + side

            @pl.when(z == owner)
            def _():
                trace_own(side, p).wait()

            @pl.when(z != owner)
            def _():
                trace_copy(side, p, 0).wait_recv()

    def pick(p, g):
        sub = sublanes()
        at = jnp.broadcast_to(points[pl.ds(g, 1), :], (8, 128)) - strip * 4096
        tile, lane = (at >> 3) & 3, (at & 96) | ((at >> 7) & 31)
        hit = ((at >> 12) == 0) & ((at & 7) == sub)
        rows = jnp.zeros((8, 128), F32) if p == 0 else picked[g]
        for side in range(2):
            for c in range(2):
                got = [jnp.take_along_axis(tbuf[side, p, c, t], lane, axis=1) for t in range(MAIN)]
                best = got[0]
                for t in range(1, MAIN):
                    best = jnp.where(tile == t, got[t], best)
                one = jnp.sum(jnp.where(hit, best, 0.0), axis=0, keepdims=True)
                rows = jnp.where(sub == side * 4 + p * 2 + c, jnp.broadcast_to(one, (8, 128)), rows)
        picked[g] = rows

    def pick_all(p):
        def four(i, carry):
            for n in range(4):
                pick(p, 4 * i + n)
            return carry

        lax.fori_loop(0, 4, four, 0)

    def picked_copy(j, source, to):
        return pltpu.make_async_remote_copy(
            src_ref=picked.at[to // 2], dst_ref=gat.at[source], send_sem=gs.at[j], recv_sem=gr.at[j],
            device_id=in_plane(to), device_id_type=MESH,
        )

    picked_own = pltpu.make_async_copy(picked.at[place // 2], gat.at[place], gown)

    def pick_send():
        pick_all(1)
        for j in range(1, PLANE):
            picked_copy(j, place, lax.rem(place + j, PLANE)).start()
        picked_own.start()

    def compress():
        for j in range(1, PLANE):
            picked_copy(j, lax.rem(place + PLANE - j, PLANE), lax.rem(place + j, PLANE)).wait_recv()
        picked_own.wait()
        lane32 = lax.broadcasted_iota(jnp.int32, (32, 128), 1)
        row32 = lax.broadcasted_iota(jnp.int32, (32, 128), 0)
        odd = jnp.full((8, 128), lax.rem(strip, 2) == 1)
        for m in range(GROUP):
            tile = (gat[4 * m] + gat[4 * m + 1]) + (gat[4 * m + 2] + gat[4 * m + 3])
            tile = jnp.where(odd, pltpu.roll(tile, 64, 1), tile)
            tile = jnp.where(lanes() < 64, tile, 0.0)
            for side in range(2):
                mats[side, 4 * m : 4 * m + 4, :] = tile[4 * side : 4 * side + 4, :]
        augmented = []
        for side in range(2):
            mat = mats[side]
            zero = jnp.zeros((32, 128), F32)
            spread = jnp.concatenate([zero, zero, mat, zero], axis=0)
            gram = lax.dot_general(
                mat, spread, (((1,), (1,)), ((), ())), precision=lax.Precision.HIGHEST, preferred_element_type=F32
            )
            augmented.append(jnp.where(lane32 < 64, mat, gram))
        for first in range(0, 32, BLOCK):
            spread = [
                [jnp.broadcast_to(a[:, 64 + k : 65 + k], (32, 128)) for k in range(first, first + BLOCK)] for a in augmented
            ]
            for j in range(BLOCK):
                k = first + j
                for side in range(2):
                    a, columns = augmented[side], spread[side]
                    inverse = lax.rsqrt(jnp.broadcast_to(columns[j][k : k + 1, :], (32, 128)))
                    row = jnp.broadcast_to(a[k : k + 1, :], (32, 128)) * inverse
                    column = columns[j] * inverse
                    augmented[side] = jnp.where(row32 > k, a - column * row, jnp.where(row32 == k, row, a))
                    for i in range(j + 1, BLOCK):
                        across = jnp.broadcast_to(columns[i][k : k + 1, :], (32, 128)) * inverse
                        columns[i] = columns[i] - column * across
        for side in range(2):
            bases[side] = augmented[side][:, :BS]

    later = iter(range(len(early), len(queue)))

    def take(n):
        for _ in range(n):
            advance(next(later))

    take(TAKE[0])
    source_row(0)
    take(TAKE[1])
    for step in range(2, ITERS + 1):
        sweep(0, step)
        take(TAKE[step])
    trace_send(0)
    send_back(0)
    halo_wait(1)
    source_row(1, jnp.where(z == 3, 3, 0), 5)

    @pl.when((z == 3) | (z == 4))
    def _():
        for step in range(2, ITERS + 1):
            sweep(1, step, jnp.where(z == 3, HALO + OWN - 1, HALO))
        trace_send(1)

    source_row(1, jnp.where(z == 3, 0, 5), 3)
    for step in range(2, ITERS + 1):
        sweep(1, step)
    send_back(1)
    trace_wait(0)
    pick_all(0)
    trace_wait(1)
    pick_send()
    receive_back(0)
    receive_back(1)
    compress()

    for j in range(1, GROUP):
        for p in range(PAIR):
            f_copy(p, j, me, peer_of(j)).wait_send()
            back_copy(p, j, me, peer_of(j)).wait_send()
        s_copy(j, me, peer_of(j)).wait_send()
        e_copy(j, me, peer_of(j)).wait_send()
    for k in range(4):
        for j in range(GROUP):
            m = from_of(j)

            @pl.when((m < 4) & (z > 0))
            def _():
                up_copy(k, j, m).wait_send()

            @pl.when((m >= 4) & (z < 7))
            def _():
                down_copy(k, j, m).wait_send()

    for p in range(PAIR):
        for side in range(2):

            @pl.when(z == 3 + side)
            def _():
                for other in range(8):
                    if other != 3 + side:
                        trace_copy(side, p, other).wait_send()

    for j in range(1, PLANE):
        picked_copy(j, place, lax.rem(place + j, PLANE)).wait_send()


def swept(probes, slow, absorb, partition):
    far = pl.BlockSpec(memory_space=pltpu.HBM)
    near = pl.BlockSpec(memory_space=pltpu.VMEM)
    dma = pltpu.SemaphoreType.DMA
    return pl.pallas_call(
        kernel,
        out_shape=(
            jax.ShapeDtypeStruct((2 * PROBES * 64, 128), F32),
            jax.ShapeDtypeStruct((2, 2 * PROBES, BS), F32),
        ),
        in_specs=[far] * 4,
        out_specs=(near, near),
        scratch_shapes=[
            pltpu.VMEM((2 * PROBES * 64, 128), F32),
            pltpu.VMEM((64, 128), F32),
            pltpu.SMEM((2,), jnp.int32),
            pltpu.VMEM((2, 8, 128), F32),
            pltpu.VMEM((2, 8, 128), F32),
            pltpu.VMEM((PAIR, GROUP, 2, 2, MAIN, 8, 128), F32),
            pltpu.VMEM((2, MAIN, 8, 128), F32),
            pltpu.VMEM((4, 8, 128), F32),
            pltpu.VMEM((PAIR, ROWS, 2, MAIN, 8, 128), F32),
            pltpu.VMEM((ROWS, MAIN, 8, 128), F32),
            pltpu.VMEM((ROWS // 2, 4, 8, 128), F32),
            pltpu.VMEM((ROWS, 2, POS, 128), F32),
            pltpu.VMEM((PAIR, ROWS, 2, POS, 128), F32),
            pltpu.VMEM((PAIR, ROWS, 2, POS, 128), F32),
            pltpu.VMEM((PAIR, ROWS, 2, POS, 128), F32),
            pltpu.VMEM((PAIR, OWN, 2, MAIN, 8, 128), F32),
            pltpu.VMEM((PROBES, 2, 2, MAIN, 8, 128), F32),
            pltpu.VMEM((16, 128), jnp.int32),
            pltpu.VMEM((2, MAIN, 8, 128), F32),
            pltpu.VMEM((2, PAIR, 2, MAIN, 8, 128), F32),
            pltpu.VMEM((16, 8, 128), F32),
            pltpu.VMEM((PLANE, 8, 128), F32),
            pltpu.VMEM((2, 32, 128), F32),
            dma((4,)),
            dma((2,)),
            dma((2,)),
            dma((6,)),
            dma((4, GROUP)),
            dma((4, GROUP)),
            dma((4, GROUP)),
            dma((4, GROUP)),
            dma((PAIR, GROUP)),
            dma((PAIR, GROUP)),
            dma((PAIR, 8)),
            dma((2, PAIR)),
            dma((PAIR,)),
            dma((PLANE,)),
            dma((PLANE,)),
            dma(()),
        ],
        compiler_params=pltpu.CompilerParams(
            collective_id=1, has_side_effects=True, vmem_limit_bytes=VMEM_LIMIT
        ),
        name="sweeps",
    )(probes, slow, absorb, partition)


def per_device(probes, slowness, absorbing, partition):
    flat = probes.reshape(PROBES, 2, 2, 32, 128).transpose(0, 1, 3, 2, 4).reshape(2 * PROBES * 64, 128)
    slow = slowness.reshape(2, 32, 128).transpose(1, 0, 2).reshape(64, 128)
    out, bases = swept(flat, slow, absorbing, partition.reshape(128, 128))
    field = out.reshape(PROBES, 2, 32, 2, 128).transpose(0, 1, 3, 2, 4).reshape(PROBES, 2, 2, 4096)
    return field, bases[None]


def solution(mesh):
    return jax.shard_map(
        per_device,
        mesh=mesh,
        in_specs=(P(None, None, "layer", "strip"), P("layer", "strip"), P("layer"), P()),
        out_specs=(P(None, None, "layer", "strip"), P(("layer", "strip"), None, None, None)),
        check_vma=False,
    )
```
